512 devices in a mesh: seq: 16 (over y_lo, x, core), pair: 32 (over y_hi, z).
Axes of the slice: x: 4, y: 4 (y_hi: 2, y_lo: 2; y = y_hi * 2 + y_lo), z: 16, core: 2. Of those that a mesh axis runs over, the one named last changes fastest.
Arguments:
- queries: bfloat16 [32, 2048, 1792], P('pair', 'seq'), may hold values from -6 to 6
- keys_values: bfloat16 [32, 2048, 512], P('pair', 'seq'), may hold values from -6 to 6
- cotangent: bfloat16 [32, 2048, 1792], P('pair', 'seq'), may hold values from -6 to 6
- resp_len: int32 [32, 2], P('pair'), may hold values from 128 to 512, as said below
- query_bias: float32 [1792], replicated, may hold values from -3 to 3
Outputs:
- grad_queries: float32 [32, 2048, 1792], P('pair', 'seq')
- grad_keys_values: float32 [32, 2048, 512], P('pair', 'seq')
- grad_bias_q: float32 [1792], replicated
- grad_bias_v: float32 [256], replicated
The draws below stay inside these ranges and needn't reach their ends.
Inputs may be any that keep to these rules, and one draw needn't show every extreme that they name: `resp_len`: in every pair one of the two lengths equals 512.
All inputs are finite; a program needn't handle non-finite values.
Results may differ from the reference program's by a relative error of at most 0.035.
Values may be sent and summed in bfloat16 or wider, within the bound.
A program may use at most 64 MiB of HBM per device.

```python
import math
import jax
import jax.numpy as jnp
from jax import lax

P_DEV = 64
R_DEV = 32
QUERY_HEADS = 14
KEY_VALUE_HEADS = 2
HEAD_SIZE = 128
PAIR_ROWS = 2048
RESP = 512
PREFERENCE_PAIRS = 32


def draw_queries(key, part):
    key = jax.random.fold_in(key, 1)
    base_offset = jnp.clip(1.5 * jax.random.normal(key, (PREFERENCE_PAIRS, PAIR_ROWS, QUERY_HEADS * HEAD_SIZE), jnp.float32), -6.0, 6.0)
    return base_offset.astype(jnp.bfloat16)


def draw_keys_values(key, part):
    key = jax.random.fold_in(key, 2)
    base_offset = jnp.clip(1.5 * jax.random.normal(key, (PREFERENCE_PAIRS, PAIR_ROWS, 2 * KEY_VALUE_HEADS * HEAD_SIZE), jnp.float32), -6.0, 6.0)
    return base_offset.astype(jnp.bfloat16)


def draw_resp_len(key, part):
    key = jax.random.fold_in(key, 3)
    first_index, second = jax.random.split(key)
    other = jax.random.randint(first_index, (PREFERENCE_PAIRS,), RESP // 4, RESP + 1)
    which = jax.random.randint(second, (PREFERENCE_PAIRS,), 0, 2)
    chosen = jnp.where(which == 0, RESP, other)
    rejected = jnp.where(which == 1, RESP, other)
    return jnp.stack([chosen, rejected], -1).astype(jnp.int32)


def levels(rng, extent, pieces, least, largest):
    gain, own = 1.0, jax.random.fold_in(rng, 6)
    for position, blocks in pieces:
        draws = jnp.exp(jax.random.uniform(jax.random.fold_in(own, position), (blocks,), jnp.float32, least / len(pieces), largest / len(pieces)))
        gain = gain * jnp.repeat(draws, extent[position] // blocks).reshape([-1 if axis == position else 1 for axis in range(len(extent))])
    return gain


def scatter_about(stream_key, extent, spread, bound, shards=(), kind=jnp.bfloat16):
    values = jax.random.normal(stream_key, extent, jnp.float32) * spread
    if len(shards) > 0:
        values = levels(stream_key, extent, shards, -0.22, 0.18) * values
    return jnp.clip(values, min=-bound, max=bound).astype(kind)


def setup_inputs(seed: int = 0) -> dict:
    key_of = jax.random.split(jax.random.key(seed), 6)
    queries = draw_queries(jax.random.fold_in(key_of[5], 71), 0)
    keys_values = draw_keys_values(jax.random.fold_in(key_of[5], 71), 0)
    cotangent = scatter_about(key_of[2], (PREFERENCE_PAIRS, PAIR_ROWS, QUERY_HEADS * HEAD_SIZE), 1.0, 6.0, ((0, 32), (1, 16)))
    resp_len = draw_resp_len(jax.random.fold_in(key_of[5], 71), 0)
    query_bias = scatter_about(key_of[4], (QUERY_HEADS * HEAD_SIZE,), 0.5, 3.0, (), jnp.float32)
    return dict(queries=queries, keys_values=keys_values, cotangent=cotangent, resp_len=resp_len, query_bias=query_bias)


def row_layout(row_block, prompt_dev, resp_dev):
    window_length = prompt_dev + 2 * resp_dev
    block_tile = row_block // window_length
    offset = row_block % window_length
    kind = jnp.where(offset < prompt_dev, 0, jnp.where(offset < prompt_dev + resp_dev, 1, 2)).astype(jnp.int32)
    place = jnp.where(kind == 0, block_tile * prompt_dev + offset, block_tile * resp_dev + offset - prompt_dev - (kind - 1) * resp_dev)
    return (kind, place.astype(jnp.int32))

def visible(q_kind, q_place, k_kind, k_place, lengths):
    k_limit = jnp.where(k_kind == 1, lengths[0], lengths[1])
    causal = k_place <= q_place
    from_prompt = (k_kind == 0) & ((q_kind != 0) | causal)
    from_reply = (k_kind == q_kind) & (k_kind != 0) & causal & (k_place < k_limit)
    return from_prompt | from_reply

def live_rows(kind, place, lengths):
    limit = jnp.where(kind == 1, lengths[0], lengths[1])
    return (kind == 0) | (place < limit)

def one_pair(items, query_bias):
    queries, keys_values, cotangent, lengths = items
    query_group = QUERY_HEADS // KEY_VALUE_HEADS
    scale = 1.0 / math.sqrt(HEAD_SIZE)
    row_block = queries.shape[0]
    index = jnp.arange(row_block, dtype=jnp.int32)
    kind, place = row_layout(index, P_DEV, R_DEV)
    allow = visible(kind[:, None], place[:, None], kind[None, :], place[None, :], lengths)[:, None, None, :]
    valid_mask = live_rows(kind, place, lengths)
    query_lower = (queries.astype(jnp.float32) + query_bias).astype(jnp.bfloat16)
    query_head_rows = query_lower.astype(jnp.float32).reshape(row_block, KEY_VALUE_HEADS, query_group, HEAD_SIZE)
    key_rows = keys_values[:, :KEY_VALUE_HEADS * HEAD_SIZE].astype(jnp.float32).reshape(row_block, KEY_VALUE_HEADS, HEAD_SIZE)
    value_rows = keys_values[:, KEY_VALUE_HEADS * HEAD_SIZE:].astype(jnp.float32).reshape(row_block, KEY_VALUE_HEADS, HEAD_SIZE)
    scores = jnp.einsum('qhgd,khd->qhgk', query_head_rows, key_rows) * scale
    scores = jnp.where(allow, scores, jnp.float32(-1e+30))
    top = scores.max(-1)
    expo = jnp.where(allow, jnp.exp(scores - top[..., None]), jnp.float32(0.0))
    total = expo.sum(-1)
    weights = lax.optimization_barrier(expo.astype(jnp.bfloat16)).astype(jnp.float32)
    attended = (jnp.einsum('qhgk,khd->qhgd', weights, value_rows) / total[..., None]).astype(jnp.bfloat16)
    output_gradient = jnp.where(valid_mask[:, None], cotangent, jnp.zeros_like(cotangent)).reshape(row_block, KEY_VALUE_HEADS, query_group, HEAD_SIZE)
    output_gradient = output_gradient.astype(jnp.float32)
    row_dot = lax.optimization_barrier(jnp.sum(output_gradient * attended.astype(jnp.float32), -1))
    prob = expo / total[..., None]
    prob_low = lax.optimization_barrier(prob.astype(jnp.bfloat16)).astype(jnp.float32)
    value_gradient = jnp.einsum('njma,njmv->ajv', prob_low, output_gradient).reshape(row_block, KEY_VALUE_HEADS * HEAD_SIZE)
    grad_prob = jnp.einsum('qhgd,khd->qhgk', output_gradient, value_rows)
    score_gradient = (prob * (grad_prob - row_dot[..., None]) * scale).astype(jnp.bfloat16)
    score_gradient = lax.optimization_barrier(score_gradient).astype(jnp.float32)
    dq = jnp.einsum('qhgk,khd->qhgd', score_gradient, key_rows).reshape(row_block, QUERY_HEADS * HEAD_SIZE)
    key_gradient = jnp.einsum('njma,njmv->ajv', score_gradient, query_head_rows).reshape(row_block, KEY_VALUE_HEADS * HEAD_SIZE)
    key_value_gradient = jnp.concatenate([key_gradient, value_gradient], 1)
    return (dq, key_value_gradient, dq.sum(0), value_gradient.sum(0))

def reference(queries, keys_values, cotangent, resp_len, query_bias):
    grad_q, key_value_gradient, sums_q, sums_v = lax.map(lambda items: one_pair(items, query_bias), (queries, keys_values, cotangent, resp_len))
    return (grad_q, key_value_gradient, sums_q.sum(0), sums_v.sum(0))
```

```python
import functools
import math

import jax
import jax.numpy as jnp
from jax import lax
from jax.experimental import pallas as pl
from jax.experimental.pallas import tpu as pltpu
from jax.sharding import PartitionSpec as P

HEADS = 7
DIM = 128
ROWS = 128
LANES = HEADS * 2 * ROWS
RLANES = HEADS * ROWS
UNITS = 4
SCALE = 1.0 / math.sqrt(DIM)
C2 = SCALE * math.log2(math.e)
NEG = -1e30
MESH = pl.DeviceIdType.MESH
F32, BF16 = jnp.float32, jnp.bfloat16


def xor(value, mask):
    out = value
    bit = 1
    while bit <= mask:
        if mask & bit:
            out = out + bit - 2 * bit * ((value // bit) % 2)
        bit *= 2
    return out


def dot_nt(a, b):
    return lax.dot_general(a, b, (((1,), (1,)), ((), ())), preferred_element_type=F32)


def dot(a, b):
    return jnp.dot(a, b, preferred_element_type=F32)


def kernel(
    pair_near,
    pair_far,
    q_hbm,
    kv_hbm,
    cot_hbm,
    len_ref,
    bias_ref,
    dq_hbm,
    dkv_ref,
    bq_ref,
    bv_ref,
    kvs,
    kvg,
    qin,
    doin,
    qcat,
    docat,
    bq3,
    bdo3,
    kp,
    vp,
    k3,
    v3,
    kt,
    kt3,
    bias12,
    bias3,
    prob,
    gprob,
    prob3,
    gprob3,
    st,
    st3,
    wrow,
    pb,
    dsb,
    p3b,
    ds3b,
    stage,
    rs,
    dqst,
    vec,
    ar1,
    ar2,
    ar3,
    ar4,
    loc_sem,
    kv_send,
    kv_recv,
    x_send,
    x_recv,
    rs_send,
    rs_recv,
    dq_sem,
    a_send,
    a_recv,
):
    s = lax.axis_index("seq")
    p = lax.axis_index("pair")
    chip = s // 2
    core = s % 2
    other = 1 - core
    duo = s // 4
    near, far = pair_near, pair_far

    def seq_dev(m):
        return {"seq": xor(s, m), "pair": p}

    def pair_dev(n):
        return {"seq": s, "pair": xor(p, n)}

    own_cols = pl.ds(pl.multiple_of(core * RLANES, 128), RLANES)
    other_cols = pl.ds(pl.multiple_of(other * RLANES, 128), RLANES)

    local = []
    for h in range(2):
        for part in range(2):
            local.append(
                pltpu.make_async_copy(
                    kv_hbm.at[:, pl.ds((2 * part + h) * DIM, DIM)],
                    kvs.at[h, part],
                    loc_sem.at[2 * h + part],
                )
            )
    local.append(pltpu.make_async_copy(q_hbm.at[:, own_cols], qin.at[core], loc_sem.at[4]))
    local.append(pltpu.make_async_copy(cot_hbm.at[:, own_cols], doin.at[core], loc_sem.at[5]))
    for cp in local:
        cp.start()

    barrier = pltpu.get_barrier_semaphore()
    for m in range(1, 16):
        pl.semaphore_signal(barrier, inc=1, device_id=seq_dev(m), device_id_type=MESH)
    for n in near + far:
        pl.semaphore_signal(barrier, inc=1, device_id=pair_dev(n), device_id_type=MESH)
    for cp in local[:4]:
        cp.wait()
    pl.semaphore_wait(barrier, 15 + len(near) + len(far))

    def remote(src, dst, send, recv, dev):
        return pltpu.make_async_remote_copy(
            src_ref=src,
            dst_ref=dst,
            send_sem=send,
            recv_sem=recv,
            device_id=dev,
            device_id_type=MESH,
        )

    qx = remote(q_hbm.at[:, other_cols], qin.at[core], x_send.at[0], x_recv.at[0], seq_dev(1))
    dx = remote(cot_hbm.at[:, other_cols], doin.at[core], x_send.at[1], x_recv.at[1], seq_dev(1))
    qx.start()
    dx.start()
    pushes = []
    for m in range(1, 16):
        head = xor(s, m) % 2
        cp = remote(kvs.at[head], kvg.at[s], kv_send.at[m], kv_recv.at[m], seq_dev(m))
        cp.start()
        pushes.append(cp)
    kvg[s] = kvs[core]

    len0, len1 = len_ref[0, 0], len_ref[0, 1]
    key = lax.broadcasted_iota(jnp.int32, (256, 128), 0)
    lane = lax.broadcasted_iota(jnp.int32, (256, 128), 1)
    bias12[...] = jnp.where(key + 256 * duo <= lane + 128 * chip, 0.0, NEG).astype(F32)
    key = lax.broadcasted_iota(jnp.int32, (128, 128), 0)
    lane = lax.broadcasted_iota(jnp.int32, (128, 128), 1)
    place_q = jnp.where(lane < 64, lane, lane - 64) + 64 * chip
    limit = jnp.where(lane < 64, len0, len1)
    for u in range(UNITS):
        place_k = key + 128 * xor(duo, u)
        seen = (place_k <= place_q) & (place_k < limit)
        bias3[u] = jnp.where(seen, 0.0, NEG).astype(F32)

    bq3[...] = jnp.zeros_like(bq3)
    bdo3[...] = jnp.zeros_like(bdo3)
    row = lax.broadcasted_iota(jnp.int32, (32, 128), 0)

    def prepare(blk):
        base = 32 * (2 * chip + blk)
        for h in range(HEADS):
            cols = pl.ds(h * DIM, DIM)
            bias = bias_ref[:, pl.ds(pl.multiple_of((core * HEADS + h) * DIM, 128), DIM)]
            x = (qin[blk, :, cols].astype(F32) + bias).astype(BF16)
            d = doin[blk, :, cols]
            d1 = jnp.where(row + base < len0, d[64:96].astype(F32), 0.0).astype(BF16)
            d2 = jnp.where(row + base < len1, d[96:128].astype(F32), 0.0).astype(BF16)
            for cat, block, y0, y1, y2 in (
                (qcat, bq3, x[0:64], x[64:96], x[96:128]),
                (docat, bdo3, d[0:64], d1, d2),
            ):
                at = h * 256
                cat[pl.ds(at + 64 * blk, 64), :] = y0
                cat[pl.ds(at + 128 + 32 * blk, 32), :] = y1
                cat[pl.ds(at + 192 + 32 * blk, 32), :] = y2
                block[pl.ds(h * 128 + 32 * blk, 32), pl.ds(0, 128)] = y1
                block[pl.ds(h * 128 + 64 + 32 * blk, 32), pl.ds(128, 128)] = y2

    for cp in local[4:]:
        cp.wait()
    qx.wait_recv()
    dx.wait_recv()
    prepare(0)
    prepare(1)

    def gather_unit(u):
        for m in range(4 * u, 4 * u + 4):
            if m:
                pushes[m - 1].wait_recv()
        first = 4 * xor(duo, u)

        def rows(part, start, size):
            return jnp.concatenate(
                [kvg[first + b, part, pl.ds(start, size), :] for b in range(4)], 0
            )

        kp[u] = rows(0, 0, 64)
        vp[u] = rows(1, 0, 64)
        k3[u, :, 0:128] = rows(0, 64, 32)
        k3[u, :, 128:256] = rows(0, 96, 32)
        v3[u, :, 0:128] = rows(1, 64, 32)
        v3[u, :, 128:256] = rows(1, 96, 32)
        kt[:, pl.ds(256 * u, 256)] = kp[u].astype(F32).T.astype(BF16)
        kt3[:, pl.ds(128 * u, 128)] = k3[u].astype(F32).T.astype(BF16)

    def phase_a(u):
        gather_unit(u)
        earlier = xor(duo, u) < duo

        @pl.loop(0, HEADS)
        def _(h):
            at = pl.multiple_of(h * 256, 256)
            at3 = pl.multiple_of(h * 128, 128)
            rows = pl.ds(at, 256)
            rows3 = pl.ds(at3, 128)
            sc = dot_nt(kp[u], qcat[rows, :])
            if u == 0:
                sc = jnp.concatenate([sc[:, :128] + bias12[...], sc[:, 128:]], 1)
            top = jnp.max(sc, 0, keepdims=True)
            pr = jnp.exp2((sc - top) * C2)
            gp = dot_nt(vp[u], docat[rows, :])
            prob[u, :, rows] = pr
            gprob[u, :, rows] = gp
            if u:
                lane1 = lax.broadcasted_iota(jnp.int32, (1, 256), 1)
                top = jnp.where((lane1 >= 128) | earlier, top, NEG)
            st[u, 0:1, rows] = top
            st[u, 1:2, rows] = jnp.sum(pr, 0, keepdims=True)
            st[u, 2:3, rows] = jnp.sum(pr * gp, 0, keepdims=True)

            sc3 = dot_nt(k3[u], bq3[rows3, :]) + bias3[u]
            top3 = jnp.max(sc3, 0, keepdims=True)
            pr3 = jnp.exp2((sc3 - top3) * C2)
            gp3 = dot_nt(v3[u], bdo3[rows3, :])
            prob3[u, :, rows3] = pr3
            gprob3[u, :, rows3] = gp3
            st3[u, 0:1, rows3] = top3
            st3[u, 1:2, rows3] = jnp.sum(pr3, 0, keepdims=True)
            st3[u, 2:3, rows3] = jnp.sum(pr3 * gp3, 0, keepdims=True)

    for u in range(UNITS):
        phase_a(u)

    @pl.loop(0, HEADS)
    def _(h):
        rows = pl.ds(pl.multiple_of(h * 256, 256), 256)
        rows3 = pl.ds(pl.multiple_of(h * 128, 128), 128)
        zero = jnp.zeros((1, 128), F32)
        tops = [st[u, 0:1, rows] for u in range(UNITS)]
        tops3 = [st3[u, 0:1, rows3] for u in range(UNITS)]
        top = functools.reduce(jnp.maximum, tops)
        top_r = functools.reduce(jnp.maximum, tops3, top[:, 128:])
        top = jnp.concatenate([top[:, :128], top_r], 1)
        part = [jnp.exp2((t - top) * C2) for t in tops]
        part3 = [jnp.exp2((t - top_r) * C2) for t in tops3]
        total = sum(st[u, 1:2, rows] * part[u] for u in range(UNITS))
        total3 = sum(st3[u, 1:2, rows3] * part3[u] for u in range(UNITS))
        rdot = sum(st[u, 2:3, rows] * part[u] for u in range(UNITS))
        rdot3 = sum(st3[u, 2:3, rows3] * part3[u] for u in range(UNITS))
        inv = 1.0 / (total + jnp.concatenate([zero, total3], 1))
        rdot = (rdot + jnp.concatenate([zero, rdot3], 1)) * inv
        wrow[0:1, rows] = rdot
        for u in range(UNITS):
            st[u, 0:1, rows] = part[u] * inv
            st3[u, 0:1, rows3] = part3[u] * inv[:, 128:]

    sends = [None]
    vsum = jnp.zeros((1, 128), F32)
    back = {}
    for u in reversed(range(UNITS)):

        @pl.loop(0, HEADS)
        def _(h):
            at = pl.multiple_of(h * 256, 256)
            rows = pl.ds(at, 256)
            rows3 = pl.ds(pl.multiple_of(h * 128, 128), 128)
            rdot = wrow[0:1, rows]
            pr = prob[u, :, rows] * st[u, 0:1, rows]
            pb[:, rows] = pr.astype(BF16)
            dsb[pl.ds(256 * u, 256), rows] = (pr * (gprob[u, :, rows] - rdot)).astype(BF16)
            pr3 = prob3[u, :, rows3] * st3[u, 0:1, rows3]
            p3b[:, rows3] = pr3.astype(BF16)
            ds3b[pl.ds(128 * u, 128), rows3] = (
                pr3 * (gprob3[u, :, rows3] - rdot[:, 128:])
            ).astype(BF16)

        dv = dot(pb[...], docat[...])
        dv3 = dot(p3b[...], bdo3[...])
        dk = dot(dsb[pl.ds(256 * u, 256), :], qcat[...]) * SCALE
        dk3 = dot(ds3b[pl.ds(128 * u, 128), :], bq3[...]) * SCALE
        vsum = vsum + jnp.sum(dv, 0, keepdims=True)
        both = jnp.sum(dv3, 0, keepdims=True)
        vsum = vsum + both[:, :128] + both[:, 128:]
        for b in range(4):
            for col, big, small in ((0, dk, dk3), (128, dv, dv3)):
                cols = pl.ds(col, 128)
                stage[u, b, 0:64, cols] = big[64 * b : 64 * b + 64].astype(BF16)
                stage[u, b, 64:96, cols] = small[32 * b : 32 * b + 32, :128].astype(BF16)
                stage[u, b, 96:128, cols] = small[32 * b : 32 * b + 32, 128:].astype(BF16)
        for m in reversed(range(4 * u, 4 * u + 4)):
            if m:
                cp = remote(
                    stage.at[u, xor(s, m) % 4],
                    rs.at[m],
                    rs_send.at[m],
                    rs_recv.at[m],
                    seq_dev(m),
                )
                cp.start()
                back[m] = cp

    vec[7:8, :] = vsum
    lane = lax.broadcasted_iota(jnp.int32, (128, 128), 1)
    for h in range(HEADS):
        rows = pl.ds(h * 256, 256)
        rows3 = pl.ds(h * 128, 128)
        dqt = dot(kt[...], dsb[:, rows])
        dqt3 = dot(kt3[...], ds3b[:, rows3])
        right = dqt[:, 128:] + jnp.where(lane < 64, dqt3[:128], dqt3[128:])
        left = dqt[:, :128].T * SCALE
        right = right.T * SCALE
        vec[h : h + 1, :] = jnp.sum(left + right, 0, keepdims=True)
        cols = pl.ds(h * DIM, DIM)
        for blk in range(2):
            dqst[blk, 0:64, cols] = left[64 * blk : 64 * blk + 64]
            dqst[blk, 64:96, cols] = right[32 * blk : 32 * blk + 32]
            dqst[blk, 96:128, cols] = right[64 + 32 * blk : 96 + 32 * blk]

    step1 = []
    for k in range(1, 8):
        cp = remote(vec, ar1.at[k], a_send.at[k], a_recv.at[k], seq_dev(2 * k))
        cp.start()
        step1.append(cp)
    dq_far = remote(
        dqst.at[other], dq_hbm.at[:, own_cols], dq_sem.at[0], dq_sem.at[1], seq_dev(1)
    )
    dq_far.start()
    dq_own = pltpu.make_async_copy(dqst.at[core], dq_hbm.at[:, own_cols], dq_sem.at[2])
    dq_own.start()

    total = vec[...]
    for k in range(1, 8):
        step1[k - 1].wait_recv()
        total = total + ar1[k]
    ar1[0] = total
    started = list(step1)
    at = 8
    src = ar1.at[0]
    for group, buf in ((near, ar2), (far, ar3)):
        step = []
        for k, n in enumerate(group):
            cp = remote(src, buf.at[k + 1], a_send.at[at], a_recv.at[at], pair_dev(n))
            cp.start()
            step.append(cp)
            at += 1
        for k, cp in enumerate(step):
            cp.wait_recv()
            total = total + buf[k + 1]
        buf[0] = total
        src = buf.at[0]
        started += step
    last = remote(src, ar4, a_send.at[at], a_recv.at[at], seq_dev(1))
    last.start()
    started.append(last)

    mine = stage[0, s % 4].astype(F32)
    theirs = None
    for m in reversed(range(1, 16)):
        back[m].wait_recv()
        part = rs[m].astype(F32)
        if m % 2 == 0:
            mine = mine + part
        else:
            theirs = part if theirs is None else theirs + part
    for head, value in ((core, mine), (other, theirs)):
        dkv_ref[:, pl.ds(pl.multiple_of(head * 128, 128), 128)] = value[:, :128]
        dkv_ref[:, pl.ds(pl.multiple_of(256 + head * 128, 128), 128)] = value[:, 128:]

    last.wait_recv()
    sib = ar4[...]
    for head, value in ((core, total), (other, sib)):
        for h in range(HEADS):
            at = pl.multiple_of((head * HEADS + h) * DIM, 128)
            bq_ref[:, pl.ds(at, DIM)] = value[h : h + 1]
        bv_ref[:, pl.ds(pl.multiple_of(head * DIM, 128), DIM)] = value[7:8]

    dq_own.wait()
    dq_far.wait_recv()
    dq_far.wait_send()
    qx.wait_send()
    dx.wait_send()
    for cp in pushes + list(back.values()) + started:
        cp.wait_send()


def on_device(pairs, queries, keys_values, cotangent, resp_len, query_bias):
    near = [n for n in range(1, min(pairs, 4))]
    far = [n for n in range(4, pairs, 4)]
    vm = pltpu.VMEM
    dma = pltpu.SemaphoreType.DMA
    any_spec = pl.BlockSpec(memory_space=pl.ANY)
    vmem_spec = pl.BlockSpec(memory_space=pltpu.VMEM)
    scratch = [
        vm((2, 2, 128, 128), BF16),
        vm((16, 2, 128, 128), BF16),
        vm((2, 128, RLANES), BF16),
        vm((2, 128, RLANES), BF16),
        vm((LANES, 128), BF16),
        vm((LANES, 128), BF16),
        vm((RLANES, 256), BF16),
        vm((RLANES, 256), BF16),
        vm((UNITS, 256, 128), BF16),
        vm((UNITS, 256, 128), BF16),
        vm((UNITS, 128, 256), BF16),
        vm((UNITS, 128, 256), BF16),
        vm((128, UNITS * 256), BF16),
        vm((256, UNITS * 128), BF16),
        vm((256, 128), F32),
        vm((UNITS, 128, 128), F32),
        vm((UNITS, 256, LANES), F32),
        vm((UNITS, 256, LANES), F32),
        vm((UNITS, 128, RLANES), F32),
        vm((UNITS, 128, RLANES), F32),
        vm((UNITS, 8, LANES), F32),
        vm((UNITS, 8, RLANES), F32),
        vm((8, LANES), F32),
        vm((256, LANES), BF16),
        vm((UNITS * 256, LANES), BF16),
        vm((128, RLANES), BF16),
        vm((UNITS * 128, RLANES), BF16),
        vm((UNITS, 4, 128, 256), BF16),
        vm((16, 128, 256), BF16),
        vm((2, 128, RLANES), F32),
        vm((8, 128), F32),
        vm((8, 8, 128), F32),
        vm((len(near) + 1, 8, 128), F32),
        vm((len(far) + 1, 8, 128), F32),
        vm((8, 128), F32),
        dma((6,)),
        dma((16,)),
        dma((16,)),
        dma((2,)),
        dma((2,)),
        dma((16,)),
        dma((16,)),
        dma((3,)),
        dma((24,)),
        dma((24,)),
    ]
    dq, dkv, bq, bv = pl.pallas_call(
        functools.partial(kernel, near, far),
        out_shape=(
            jax.ShapeDtypeStruct((128, 2 * RLANES), F32),
            jax.ShapeDtypeStruct((128, 512), F32),
            jax.ShapeDtypeStruct((1, 2 * RLANES), F32),
            jax.ShapeDtypeStruct((1, 256), F32),
        ),
        in_specs=[
            any_spec,
            any_spec,
            any_spec,
            pl.BlockSpec(memory_space=pltpu.SMEM),
            vmem_spec,
        ],
        out_specs=(any_spec, vmem_spec, vmem_spec, vmem_spec),
        scratch_shapes=scratch,
        compiler_params=pltpu.CompilerParams(
            collective_id=0, has_side_effects=True, vmem_limit_bytes=50 * 1024 * 1024
        ),
    )(queries[0], keys_values[0], cotangent[0], resp_len, query_bias.reshape(1, -1))
    return dq[None], dkv[None], bq.reshape(-1), bv.reshape(-1)


def solution(mesh):
    return jax.shard_map(
        functools.partial(on_device, mesh.shape["pair"]),
        mesh=mesh,
        in_specs=(
            P("pair", "seq", None),
            P("pair", "seq", None),
            P("pair", "seq", None),
            P("pair", None),
            P(),
        ),
        out_specs=(P("pair", "seq", None), P("pair", "seq", None), P(), P()),
        check_vma=False,
    )
```

```python
import functools
import math

import jax
import jax.numpy as jnp
from jax import lax
from jax.experimental import pallas as pl
from jax.experimental.pallas import tpu as pltpu
from jax.sharding import PartitionSpec as P

HEADS = 7
DIM = 128
ROWS = 128
LANES = HEADS * 2 * ROWS
RLANES = HEADS * ROWS
UNITS = 4
SCALE = 1.0 / math.sqrt(DIM)
C2 = SCALE * math.log2(math.e)
NEG = -1e30
MESH = pl.DeviceIdType.MESH
F32, BF16 = jnp.float32, jnp.bfloat16


def xor(value, mask):
    out = value
    bit = 1
    while bit <= mask:
        if mask & bit:
            out = out + bit - 2 * bit * ((value // bit) % 2)
        bit *= 2
    return out


def dot_nt(a, b):
    return lax.dot_general(a, b, (((1,), (1,)), ((), ())), preferred_element_type=F32)


def dot(a, b):
    return jnp.dot(a, b, preferred_element_type=F32)


def kernel(
    pair_near,
    pair_far,
    q_hbm,
    kv_hbm,
    cot_hbm,
    len_ref,
    bias_ref,
    dq_hbm,
    dkv_ref,
    bq_ref,
    bv_ref,
    kvs,
    kvg,
    qin,
    doin,
    qcat,
    docat,
    bq3,
    bdo3,
    kp,
    vp,
    k3,
    v3,
    kt,
    kt3,
    bias12,
    bias3,
    prob,
    gprob,
    prob3,
    gprob3,
    st,
    st3,
    wrow,
    pb,
    dsb,
    p3b,
    ds3b,
    stage,
    rs,
    dqst,
    vec,
    ar1,
    ar2,
    ar3,
    ar4,
    loc_sem,
    kv_send,
    kv_recv,
    x_send,
    x_recv,
    rs_send,
    rs_recv,
    dq_sem,
    a_send,
    a_recv,
):
    s = lax.axis_index("seq")
    p = lax.axis_index("pair")
    chip = s // 2
    core = s % 2
    other = 1 - core
    duo = s // 4
    near, far = pair_near, pair_far

    def seq_dev(m):
        return {"seq": xor(s, m), "pair": p}

    def pair_dev(n):
        return {"seq": s, "pair": xor(p, n)}

    own_cols = pl.ds(pl.multiple_of(core * RLANES, 128), RLANES)
    other_cols = pl.ds(pl.multiple_of(other * RLANES, 128), RLANES)

    local = []
    for h in range(2):
        for part in range(2):
            local.append(
                pltpu.make_async_copy(
                    kv_hbm.at[:, pl.ds((2 * part + h) * DIM, DIM)],
                    kvs.at[h, part],
                    loc_sem.at[2 * h + part],
                )
            )
    local.append(pltpu.make_async_copy(q_hbm.at[:, own_cols], qin.at[core], loc_sem.at[4]))
    local.append(pltpu.make_async_copy(cot_hbm.at[:, own_cols], doin.at[core], loc_sem.at[5]))
    for cp in local:
        cp.start()

    barrier = pltpu.get_barrier_semaphore()
    for m in range(1, 16):
        pl.semaphore_signal(barrier, inc=1, device_id=seq_dev(m), device_id_type=MESH)
    for n in near + far:
        pl.semaphore_signal(barrier, inc=1, device_id=pair_dev(n), device_id_type=MESH)
    for cp in local[:4]:
        cp.wait()
    pl.semaphore_wait(barrier, 15 + len(near) + len(far))

    def remote(src, dst, send, recv, dev):
        return pltpu.make_async_remote_copy(
            src_ref=src,
            dst_ref=dst,
            send_sem=send,
            recv_sem=recv,
            device_id=dev,
            device_id_type=MESH,
        )

    qx = remote(q_hbm.at[:, other_cols], qin.at[core], x_send.at[0], x_recv.at[0], seq_dev(1))
    dx = remote(cot_hbm.at[:, other_cols], doin.at[core], x_send.at[1], x_recv.at[1], seq_dev(1))
    qx.start()
    dx.start()
    pushes = {}

    def push(src, block, mask, to):
        cp = remote(src, kvg.at[block], kv_send.at[mask], kv_recv.at[mask], seq_dev(to))
        cp.start()
        pushes[mask] = cp

    for m in (2, 3, 6, 7, 8, 9, 1):
        push(kvs.at[xor(s, m) % 2], s, m, m)
    kvg[s] = kvs[core]

    len0, len1 = len_ref[0, 0], len_ref[0, 1]
    key = lax.broadcasted_iota(jnp.int32, (256, 128), 0)
    lane = lax.broadcasted_iota(jnp.int32, (256, 128), 1)
    bias12[...] = jnp.where(key + 256 * duo <= lane + 128 * chip, 0.0, NEG).astype(F32)
    key = lax.broadcasted_iota(jnp.int32, (128, 128), 0)
    lane = lax.broadcasted_iota(jnp.int32, (128, 128), 1)
    place_q = jnp.where(lane < 64, lane, lane - 64) + 64 * chip
    limit = jnp.where(lane < 64, len0, len1)
    for u in range(UNITS):
        place_k = key + 128 * xor(duo, u)
        seen = (place_k <= place_q) & (place_k < limit)
        bias3[u] = jnp.where(seen, 0.0, NEG).astype(F32)

    bq3[...] = jnp.zeros_like(bq3)
    bdo3[...] = jnp.zeros_like(bdo3)
    row = lax.broadcasted_iota(jnp.int32, (32, 128), 0)

    def prepare(blk):
        base = 32 * (2 * chip + blk)
        for h in range(HEADS):
            cols = pl.ds(h * DIM, DIM)
            bias = bias_ref[pl.ds(pl.multiple_of((core * HEADS + h) * DIM, 128), DIM)][None]
            x = (qin[blk, :, cols].astype(F32) + bias).astype(BF16)
            d = doin[blk, :, cols]
            d1 = jnp.where(row + base < len0, d[64:96].astype(F32), 0.0).astype(BF16)
            d2 = jnp.where(row + base < len1, d[96:128].astype(F32), 0.0).astype(BF16)
            for cat, block, y0, y1, y2 in (
                (qcat, bq3, x[0:64], x[64:96], x[96:128]),
                (docat, bdo3, d[0:64], d1, d2),
            ):
                at = h * 256
                cat[pl.ds(at + 64 * blk, 64), :] = y0
                cat[pl.ds(at + 128 + 32 * blk, 32), :] = y1
                cat[pl.ds(at + 192 + 32 * blk, 32), :] = y2
                block[pl.ds(h * 128 + 32 * blk, 32), pl.ds(0, 128)] = y1
                block[pl.ds(h * 128 + 64 + 32 * blk, 32), pl.ds(128, 128)] = y2

    for cp in local[4:]:
        cp.wait()
    qx.wait_recv()
    dx.wait_recv()
    prepare(0)
    prepare(1)

    arrivals = ((2, 3, 6, 7, 8, 9, 1), (4, 5), (10, 11), (12, 13, 14, 15))

    def relay(mask, held, to):
        push(kvg.at[xor(s, held)], xor(s, held), mask, to)

    def gather_unit(u):
        for m in arrivals[u]:
            pushes[m].wait_recv()
        if u == 0:
            relay(4, 2, 6)
            relay(5, 7, 2)
            for m, to in ((10, 2), (14, 6), (11, 2), (15, 6)):
                relay(m, m - to, to)
        elif u == 1:
            relay(12, 4, 8)
            relay(13, 5, 8)
        first = 4 * xor(duo, u)

        def rows(part, start, size):
            return jnp.concatenate(
                [kvg[first + b, part, pl.ds(start, size), :] for b in range(4)], 0
            )

        kp[u] = rows(0, 0, 64)
        vp[u] = rows(1, 0, 64)
        k3[u, :, 0:128] = rows(0, 64, 32)
        k3[u, :, 128:256] = rows(0, 96, 32)
        v3[u, :, 0:128] = rows(1, 64, 32)
        v3[u, :, 128:256] = rows(1, 96, 32)
        kt[:, pl.ds(256 * u, 256)] = kp[u].astype(F32).T.astype(BF16)
        kt3[:, pl.ds(128 * u, 128)] = k3[u].astype(F32).T.astype(BF16)

    def phase_a(u):
        gather_unit(u)
        earlier = xor(duo, u) < duo

        @pl.loop(0, HEADS, unroll=True)
        def _(h):
            at = pl.multiple_of(h * 256, 256)
            at3 = pl.multiple_of(h * 128, 128)
            rows = pl.ds(at, 256)
            rows3 = pl.ds(at3, 128)
            sc = dot_nt(kp[u], qcat[rows, :])
            if u == 0:
                sc = jnp.concatenate([sc[:, :128] + bias12[...], sc[:, 128:]], 1)
            top = jnp.max(sc, 0, keepdims=True)
            pr = jnp.exp2((sc - top) * C2)
            gp = dot_nt(vp[u], docat[rows, :])
            prob[u, :, rows] = pr
            gprob[u, :, rows] = gp
            if u:
                lane1 = lax.broadcasted_iota(jnp.int32, (1, 256), 1)
                top = jnp.where((lane1 >= 128) | earlier, top, NEG)
            st[u, 0:1, rows] = top
            st[u, 1:2, rows] = jnp.sum(pr, 0, keepdims=True)
            st[u, 2:3, rows] = jnp.sum(pr * gp, 0, keepdims=True)

            sc3 = dot_nt(k3[u], bq3[rows3, :]) + bias3[u]
            top3 = jnp.max(sc3, 0, keepdims=True)
            pr3 = jnp.exp2((sc3 - top3) * C2)
            gp3 = dot_nt(v3[u], bdo3[rows3, :])
            prob3[u, :, rows3] = pr3
            gprob3[u, :, rows3] = gp3
            st3[u, 0:1, rows3] = top3
            st3[u, 1:2, rows3] = jnp.sum(pr3, 0, keepdims=True)
            st3[u, 2:3, rows3] = jnp.sum(pr3 * gp3, 0, keepdims=True)

    for u in range(UNITS):
        phase_a(u)

    @pl.loop(0, HEADS)
    def _(h):
        rows = pl.ds(pl.multiple_of(h * 256, 256), 256)
        rows3 = pl.ds(pl.multiple_of(h * 128, 128), 128)
        zero = jnp.zeros((1, 128), F32)
        tops = [st[u, 0:1, rows] for u in range(UNITS)]
        tops3 = [st3[u, 0:1, rows3] for u in range(UNITS)]
        top = functools.reduce(jnp.maximum, tops)
        top_r = functools.reduce(jnp.maximum, tops3, top[:, 128:])
        top = jnp.concatenate([top[:, :128], top_r], 1)
        part = [jnp.exp2((t - top) * C2) for t in tops]
        part3 = [jnp.exp2((t - top_r) * C2) for t in tops3]
        total = sum(st[u, 1:2, rows] * part[u] for u in range(UNITS))
        total3 = sum(st3[u, 1:2, rows3] * part3[u] for u in range(UNITS))
        rdot = sum(st[u, 2:3, rows] * part[u] for u in range(UNITS))
        rdot3 = sum(st3[u, 2:3, rows3] * part3[u] for u in range(UNITS))
        inv = 1.0 / (total + jnp.concatenate([zero, total3], 1))
        rdot = (rdot + jnp.concatenate([zero, rdot3], 1)) * inv
        wrow[0:1, rows] = rdot
        for u in range(UNITS):
            st[u, 0:1, rows] = part[u] * inv
            st3[u, 0:1, rows3] = part3[u] * inv[:, 128:]

    def grad_scores(u):
        @pl.loop(0, HEADS, unroll=True)
        def _(h):
            at = pl.multiple_of(h * 256, 256)
            rows = pl.ds(at, 256)
            rows3 = pl.ds(pl.multiple_of(h * 128, 128), 128)
            rdot = wrow[0:1, rows]
            pr = prob[u, :, rows] * st[u, 0:1, rows]
            pb[u, :, rows] = pr.astype(BF16)
            dsb[pl.ds(256 * u, 256), rows] = (pr * (gprob[u, :, rows] - rdot)).astype(BF16)
            pr3 = prob3[u, :, rows3] * st3[u, 0:1, rows3]
            p3b[u, :, rows3] = pr3.astype(BF16)
            ds3b[pl.ds(128 * u, 128), rows3] = (
                pr3 * (gprob3[u, :, rows3] - rdot[:, 128:])
            ).astype(BF16)

    def grad_kv(u):
        dv = dot(pb[u], docat[...])
        dv3 = dot(p3b[u], bdo3[...])
        dk = dot(dsb[pl.ds(256 * u, 256), :], qcat[...]) * SCALE
        dk3 = dot(ds3b[pl.ds(128 * u, 128), :], bq3[...]) * SCALE
        for b in range(4):
            for col, big, small in ((0, dk, dk3), (128, dv, dv3)):
                cols = pl.ds(col, 128)
                stage[u, b, 0:64, cols] = big[64 * b : 64 * b + 64].astype(BF16)
                stage[u, b, 64:96, cols] = small[32 * b : 32 * b + 32, :128].astype(BF16)
                stage[u, b, 96:128, cols] = small[32 * b : 32 * b + 32, 128:].astype(BF16)

    back = []

    def part(m):
        return stage.at[m // 4, xor(s, m) % 4]

    def give(m, slot, to):
        cp = remote(part(m), rs.at[slot], rs_send.at[slot], rs_recv.at[slot], seq_dev(to))
        cp.start()
        back.append(cp)

    def landed(slot):
        remote(
            rs.at[slot], rs.at[slot], rs_send.at[slot], rs_recv.at[slot], seq_dev(1)
        ).wait_recv()

    def add(m, *slots):
        total = part(m)[...].astype(F32)
        for slot in slots:
            landed(slot)
            total = total + rs[slot].astype(F32)
        part(m)[...] = total.astype(BF16)

    def grad_queries():
        lane = lax.broadcasted_iota(jnp.int32, (128, 128), 1)
        for h in range(HEADS):
            rows = pl.ds(h * 256, 256)
            rows3 = pl.ds(h * 128, 128)
            dqt = dot(kt[...], dsb[:, rows])
            dqt3 = dot(kt3[...], ds3b[:, rows3])
            right = dqt[:, 128:] + jnp.where(lane < 64, dqt3[:128], dqt3[128:])
            left = dqt[:, :128].T * SCALE
            right = right.T * SCALE
            vec[h : h + 1, :] = jnp.sum(left + right, 0, keepdims=True)
            cols = pl.ds(h * DIM, DIM)
            for blk in range(2):
                dqst[blk, 0:64, cols] = left[64 * blk : 64 * blk + 64]
                dqst[blk, 64:96, cols] = right[32 * blk : 32 * blk + 32]
                dqst[blk, 96:128, cols] = right[64 + 32 * blk : 96 + 32 * blk]

    grad_scores(3)
    grad_kv(3)
    give(12, 0, 8)
    give(14, 2, 6)
    give(13, 1, 8)
    give(15, 3, 6)
    for u in (2, 1, 0):
        grad_scores(u)
    grad_queries()
    vec[7:8, :] = dot(jnp.ones((8, LANES), BF16), docat[...])[0:1]
    step1 = []
    for k in range(1, 8):
        cp = remote(vec, ar1.at[k], a_send.at[k], a_recv.at[k], seq_dev(2 * k))
        cp.start()
        step1.append(cp)
    grad_kv(2)
    give(10, 4, 2)
    give(11, 5, 2)
    grad_kv(1)
    give(6, 6, 6)
    dq_far = remote(
        dqst.at[other], dq_hbm.at[:, own_cols], dq_sem.at[0], dq_sem.at[1], seq_dev(1)
    )
    dq_far.start()
    dq_own = pltpu.make_async_copy(dqst.at[core], dq_hbm.at[:, own_cols], dq_sem.at[2])
    dq_own.start()
    add(4, 0)
    give(4, 7, 6)
    add(5, 1)
    give(5, 8, 2)
    total = vec[...]
    for k in range(1, 8):
        step1[k - 1].wait_recv()
        total = total + ar1[k]
    ar1[0] = total
    started = list(step1)

    def to_pairs(group, buf, at, src):
        step = []
        for k, n in enumerate(group):
            cp = remote(src, buf.at[k + 1], a_send.at[at + k], a_recv.at[at + k], pair_dev(n))
            cp.start()
            step.append(cp)
        started.extend(step)
        return step

    def from_pairs(step, buf, total):
        for k, cp in enumerate(step):
            cp.wait_recv()
            total = total + buf[k + 1]
        buf[0] = total
        return total

    step2 = to_pairs(near, ar2, 8, ar1.at[0])
    grad_kv(0)
    give(3, 9, 3)
    give(1, 10, 1)
    add(8, 2, 4)
    give(8, 11, 8)
    add(9, 3, 5)
    give(9, 12, 9)
    total = from_pairs(step2, ar2, total)
    step3 = to_pairs(far, ar3, 11, ar2.at[0])
    add(2, 7)
    give(2, 13, 2)
    add(7, 8)
    give(7, 14, 7)
    total = from_pairs(step3, ar3, total)
    last = remote(ar3.at[0], ar4, a_send.at[18], a_recv.at[18], seq_dev(1))
    last.start()
    started.append(last)

    mine = part(0)[...].astype(F32)
    for slot in (6, 11, 13):
        landed(slot)
        mine = mine + rs[slot].astype(F32)
    theirs = jnp.zeros((128, 256), F32)
    for slot in (10, 9, 12, 14):
        landed(slot)
        theirs = theirs + rs[slot].astype(F32)
    for head, value in ((core, mine), (other, theirs)):
        dkv_ref[:, pl.ds(pl.multiple_of(head * 128, 128), 128)] = value[:, :128]
        dkv_ref[:, pl.ds(pl.multiple_of(256 + head * 128, 128), 128)] = value[:, 128:]

    last.wait_recv()
    sib = ar4[...]
    for head, value in ((core, total), (other, sib)):
        for h in range(HEADS):
            at = pl.multiple_of((head * HEADS + h) * DIM, 128)
            bq_ref[pl.ds(at, DIM)] = value[h]
        bv_ref[pl.ds(pl.multiple_of(head * DIM, 128), DIM)] = value[7]

    dq_own.wait()
    dq_far.wait_recv()
    dq_far.wait_send()
    qx.wait_send()
    dx.wait_send()
    for cp in list(pushes.values()) + back + started:
        cp.wait_send()


def hand_out(*refs):
    ins, outs, sem = refs[:4], refs[4:8], refs[8]
    copies = [pltpu.make_async_copy(a, b, sem.at[i]) for i, (a, b) in enumerate(zip(ins, outs))]
    for cp in copies:
        cp.start()
    for cp in copies:
        cp.wait()


def on_device(pairs, queries, keys_values, cotangent, resp_len, query_bias):
    near = [n for n in range(1, min(pairs, 4))]
    far = [n for n in range(4, pairs, 4)]
    vm = pltpu.VMEM
    dma = pltpu.SemaphoreType.DMA
    any_spec = pl.BlockSpec(memory_space=pl.ANY)
    hbm_spec = pl.BlockSpec(memory_space=pltpu.HBM)
    vmem_spec = pl.BlockSpec(memory_space=pltpu.VMEM)
    scratch = [
        vm((2, 2, 128, 128), BF16),
        vm((16, 2, 128, 128), BF16),
        vm((2, 128, RLANES), BF16),
        vm((2, 128, RLANES), BF16),
        vm((LANES, 128), BF16),
        vm((LANES, 128), BF16),
        vm((RLANES, 256), BF16),
        vm((RLANES, 256), BF16),
        vm((UNITS, 256, 128), BF16),
        vm((UNITS, 256, 128), BF16),
        vm((UNITS, 128, 256), BF16),
        vm((UNITS, 128, 256), BF16),
        vm((128, UNITS * 256), BF16),
        vm((256, UNITS * 128), BF16),
        vm((256, 128), F32),
        vm((UNITS, 128, 128), F32),
        vm((UNITS, 256, LANES), F32),
        vm((UNITS, 256, LANES), F32),
        vm((UNITS, 128, RLANES), F32),
        vm((UNITS, 128, RLANES), F32),
        vm((UNITS, 8, LANES), F32),
        vm((UNITS, 8, RLANES), F32),
        vm((8, LANES), F32),
        vm((UNITS, 256, LANES), BF16),
        vm((UNITS * 256, LANES), BF16),
        vm((UNITS, 128, RLANES), BF16),
        vm((UNITS * 128, RLANES), BF16),
        vm((UNITS, 4, 128, 256), BF16),
        vm((16, 128, 256), BF16),
        vm((2, 128, RLANES), F32),
        vm((8, 128), F32),
        vm((8, 8, 128), F32),
        vm((len(near) + 1, 8, 128), F32),
        vm((len(far) + 1, 8, 128), F32),
        vm((8, 128), F32),
        dma((6,)),
        dma((16,)),
        dma((16,)),
        dma((2,)),
        dma((2,)),
        dma((16,)),
        dma((16,)),
        dma((3,)),
        dma((24,)),
        dma((24,)),
    ]
    shapes = (
        jax.ShapeDtypeStruct((128, 2 * RLANES), F32),
        jax.ShapeDtypeStruct((128, 512), F32),
        jax.ShapeDtypeStruct((2 * RLANES,), F32),
        jax.ShapeDtypeStruct((256,), F32),
    )
    made = pl.pallas_call(
        functools.partial(kernel, near, far),
        out_shape=shapes,
        in_specs=[
            hbm_spec,
            hbm_spec,
            hbm_spec,
            pl.BlockSpec(memory_space=pltpu.SMEM),
            vmem_spec,
        ],
        out_specs=(any_spec, vmem_spec, vmem_spec, vmem_spec),
        scratch_shapes=scratch,
        compiler_params=pltpu.CompilerParams(
            collective_id=0, has_side_effects=True, vmem_limit_bytes=63 * 1024 * 1024
        ),
    )(queries[0], keys_values[0], cotangent[0], resp_len, query_bias)
    dq, dkv, bq, bv = pl.pallas_call(
        hand_out,
        out_shape=shapes,
        in_specs=[vmem_spec] * 4,
        out_specs=(any_spec,) * 4,
        scratch_shapes=[dma((4,))],
    )(*made)
    return dq[None], dkv[None], bq, bv


def solution(mesh):
    return jax.shard_map(
        functools.partial(on_device, mesh.shape["pair"]),
        mesh=mesh,
        in_specs=(
            P("pair", "seq", None),
            P("pair", "seq", None),
            P("pair", "seq", None),
            P("pair", None),
            P(),
        ),
        out_specs=(P("pair", "seq", None), P("pair", "seq", None), P(), P()),
        check_vma=False,
    )
```

```python
import functools
import math

import jax
import jax.numpy as jnp
from jax import lax
from jax.experimental import pallas as pl
from jax.experimental.pallas import tpu as pltpu
from jax.sharding import PartitionSpec as P

HEADS = 7
DIM = 128
ROWS = 128
LANES = HEADS * 2 * ROWS
RLANES = HEADS * ROWS
UNITS = 4
SCALE = 1.0 / math.sqrt(DIM)
C2 = SCALE * math.log2(math.e)
NEG = -1e30
MESH = pl.DeviceIdType.MESH
F32, BF16 = jnp.float32, jnp.bfloat16


def xor(value, mask):
    out = value
    bit = 1
    while bit <= mask:
        if mask & bit:
            out = out + bit - 2 * bit * ((value // bit) % 2)
        bit *= 2
    return out


def dot_nt(a, b):
    return lax.dot_general(a, b, (((1,), (1,)), ((), ())), preferred_element_type=F32)


def dot(a, b):
    return jnp.dot(a, b, preferred_element_type=F32)


def kernel(
    pair_near,
    pair_far,
    q_hbm,
    kv_hbm,
    cot_hbm,
    len_hbm,
    bias_hbm,
    dq_hbm,
    dkv_ref,
    bq_ref,
    bv_ref,
    kvs,
    kvg,
    qin,
    doin,
    qcat,
    docat,
    bq3,
    bdo3,
    kp,
    vp,
    k3,
    v3,
    kt,
    kt3,
    bias12,
    bias3,
    prob,
    gprob,
    prob3,
    gprob3,
    st,
    st3,
    wrow,
    pb,
    dsb,
    p3b,
    ds3b,
    stage,
    rs,
    dqst,
    vec,
    ar1,
    ar2,
    ar3,
    res,
    len_ref,
    bias_ref,
    loc_sem,
    kv_send,
    kv_recv,
    x_send,
    x_recv,
    rs_send,
    rs_recv,
    dq_sem,
    a_send,
    a_recv,
    b_recv,
    go_sem,
):
    s = lax.axis_index("seq")
    p = lax.axis_index("pair")
    chip = s // 2
    core = s % 2
    other = 1 - core
    duo = s // 4
    near, far = pair_near, pair_far

    def seq_dev(m):
        return {"seq": xor(s, m), "pair": p}

    def pair_dev(n):
        return {"seq": s, "pair": xor(p, n)}

    own_cols = pl.ds(pl.multiple_of(core * RLANES, 128), RLANES)
    other_cols = pl.ds(pl.multiple_of(other * RLANES, 128), RLANES)

    local = []
    for h in range(2):
        for part in range(2):
            local.append(
                pltpu.make_async_copy(
                    kv_hbm.at[:, pl.ds((2 * part + h) * DIM, DIM)],
                    kvs.at[h, part],
                    loc_sem.at[2 * h + part],
                )
            )
    local.append(pltpu.make_async_copy(q_hbm.at[:, own_cols], qin.at[core], loc_sem.at[4]))
    local.append(pltpu.make_async_copy(cot_hbm.at[:, own_cols], doin.at[core], loc_sem.at[5]))
    local.append(pltpu.make_async_copy(bias_hbm, bias_ref, loc_sem.at[6]))
    local.append(pltpu.make_async_copy(len_hbm, len_ref, loc_sem.at[7]))
    for cp in local:
        cp.start()

    barrier = pltpu.get_barrier_semaphore()

    @pl.when(core == 0)
    def _():
        for m in (2, 6, 8):
            pl.semaphore_signal(barrier, inc=1, device_id=seq_dev(m), device_id_type=MESH)

    @pl.when(core == 1)
    def _():
        for m in (3, 7, 9, 1):
            pl.semaphore_signal(barrier, inc=1, device_id=seq_dev(m), device_id_type=MESH)
        for n in near + far:
            pl.semaphore_signal(barrier, inc=1, device_id=pair_dev(n), device_id_type=MESH)

    for cp in local[:4]:
        cp.wait()

    @pl.when(core == 0)
    def _():
        pl.semaphore_wait(barrier, 7)
        pl.semaphore_signal(go_sem, inc=1, device_id=seq_dev(1), device_id_type=MESH)

    @pl.when(core == 1)
    def _():
        pl.semaphore_wait(go_sem, 1)

    def remote(src, dst, send, recv, dev):
        return pltpu.make_async_remote_copy(
            src_ref=src,
            dst_ref=dst,
            send_sem=send,
            recv_sem=recv,
            device_id=dev,
            device_id_type=MESH,
        )

    pushes = {}

    def push(src, block, mask, to):
        cp = remote(src, kvg.at[block], kv_send.at[mask], kv_recv.at[mask], seq_dev(to))
        cp.start()
        pushes[mask] = cp

    for m in (2, 7, 8, 3, 6, 9, 1):
        push(kvs.at[xor(s, m) % 2], s, m, m)
    qx = remote(q_hbm.at[:, other_cols], qin.at[core], x_send.at[0], x_recv.at[0], seq_dev(1))
    dx = remote(cot_hbm.at[:, other_cols], doin.at[core], x_send.at[1], x_recv.at[1], seq_dev(1))
    qx.start()
    dx.start()
    kvg[s] = kvs[core]

    local[7].wait()
    len0, len1 = len_ref[0, 0], len_ref[0, 1]
    key = lax.broadcasted_iota(jnp.int32, (256, 128), 0)
    lane = lax.broadcasted_iota(jnp.int32, (256, 128), 1)
    bias12[...] = jnp.where(key + 256 * duo <= lane + 128 * chip, 0.0, NEG).astype(F32)
    key = lax.broadcasted_iota(jnp.int32, (128, 128), 0)
    lane = lax.broadcasted_iota(jnp.int32, (128, 128), 1)
    place_q = jnp.where(lane < 64, lane, lane - 64) + 64 * chip
    limit = jnp.where(lane < 64, len0, len1)
    for u in range(UNITS):
        place_k = key + 128 * xor(duo, u)
        seen = (place_k <= place_q) & (place_k < limit)
        bias3[u] = jnp.where(seen, 0.0, NEG).astype(F32)

    bq3[...] = jnp.zeros_like(bq3)
    bdo3[...] = jnp.zeros_like(bdo3)
    row = lax.broadcasted_iota(jnp.int32, (32, 128), 0)

    def prepare(blk):
        base = 32 * (2 * chip + blk)
        for h in range(HEADS):
            cols = pl.ds(h * DIM, DIM)
            bias = bias_ref[pl.ds(pl.multiple_of((core * HEADS + h) * DIM, 128), DIM)][None]
            x = (qin[blk, :, cols].astype(F32) + bias).astype(BF16)
            d = doin[blk, :, cols]
            d1 = jnp.where(row + base < len0, d[64:96].astype(F32), 0.0).astype(BF16)
            d2 = jnp.where(row + base < len1, d[96:128].astype(F32), 0.0).astype(BF16)
            for cat, block, y0, y1, y2 in (
                (qcat, bq3, x[0:64], x[64:96], x[96:128]),
                (docat, bdo3, d[0:64], d1, d2),
            ):
                at = h * 256
                cat[pl.ds(pl.multiple_of(at + 64 * blk, 64), 64), :] = y0
                cat[pl.ds(pl.multiple_of(at + 128 + 32 * blk, 32), 32), :] = y1
                cat[pl.ds(pl.multiple_of(at + 192 + 32 * blk, 32), 32), :] = y2
                block[pl.ds(pl.multiple_of(h * 128 + 32 * blk, 32), 32), pl.ds(0, 128)] = y1
                block[pl.ds(pl.multiple_of(h * 128 + 64 + 32 * blk, 32), 32), pl.ds(128, 128)] = y2

    def relay(held, *ways):
        pushes[held].wait_recv()
        for mask, to in ways:
            push(kvg.at[xor(s, held)], xor(s, held), mask, to)

    relay(2, (4, 6))
    relay(7, (5, 2))
    for k in (4, 5, 6):
        local[k].wait()
    prepare(core)
    relay(8, (10, 2), (14, 6))
    relay(9, (11, 2), (15, 6))
    qx.wait_recv()
    dx.wait_recv()
    prepare(other)
    more = {0: ((3,), (6,), (1,)), 1: ((4, (12, 8)), (5, (13, 8))), 2: ((10,), (11,))}
    more[3] = ((12,), (13,), (14,), (15,))

    def gather_unit(u):
        for way in more[u]:
            relay(*way)
        first = 4 * xor(duo, u)

        def rows(part, start, size):
            return jnp.concatenate(
                [kvg[first + b, part, pl.ds(start, size), :] for b in range(4)], 0
            )

        kp[u] = rows(0, 0, 64)
        vp[u] = rows(1, 0, 64)
        k3[u, :, 0:128] = rows(0, 64, 32)
        k3[u, :, 128:256] = rows(0, 96, 32)
        v3[u, :, 0:128] = rows(1, 64, 32)
        v3[u, :, 128:256] = rows(1, 96, 32)
        kt[:, pl.ds(256 * u, 256)] = kp[u].astype(F32).T.astype(BF16)
        kt3[:, pl.ds(128 * u, 128)] = k3[u].astype(F32).T.astype(BF16)

    def phase_a(u):
        gather_unit(u)
        earlier = xor(duo, u) < duo

        @pl.loop(0, HEADS, unroll=True)
        def _(h):
            at = pl.multiple_of(h * 256, 256)
            at3 = pl.multiple_of(h * 128, 128)
            rows = pl.ds(at, 256)
            rows3 = pl.ds(at3, 128)
            sc = dot_nt(kp[u], qcat[rows, :])
            if u == 0:
                sc = jnp.concatenate([sc[:, :128] + bias12[...], sc[:, 128:]], 1)
            top = jnp.max(sc, 0, keepdims=True)
            pr = jnp.exp2((sc - top) * C2)
            gp = dot_nt(vp[u], docat[rows, :])
            prob[u, :, rows] = pr
            gprob[u, :, rows] = gp
            if u:
                lane1 = lax.broadcasted_iota(jnp.int32, (1, 256), 1)
                top = jnp.where((lane1 >= 128) | earlier, top, NEG)
            st[u, 0:1, rows] = top
            st[u, 1:2, rows] = jnp.sum(pr, 0, keepdims=True)
            st[u, 2:3, rows] = jnp.sum(pr * gp, 0, keepdims=True)

            sc3 = dot_nt(k3[u], bq3[rows3, :]) + bias3[u]
            top3 = jnp.max(sc3, 0, keepdims=True)
            pr3 = jnp.exp2((sc3 - top3) * C2)
            gp3 = dot_nt(v3[u], bdo3[rows3, :])
            prob3[u, :, rows3] = pr3
            gprob3[u, :, rows3] = gp3
            st3[u, 0:1, rows3] = top3
            st3[u, 1:2, rows3] = jnp.sum(pr3, 0, keepdims=True)
            st3[u, 2:3, rows3] = jnp.sum(pr3 * gp3, 0, keepdims=True)

    for u in range(UNITS):
        phase_a(u)

    @pl.loop(0, HEADS)
    def _(h):
        rows = pl.ds(pl.multiple_of(h * 256, 256), 256)
        rows3 = pl.ds(pl.multiple_of(h * 128, 128), 128)
        zero = jnp.zeros((1, 128), F32)
        tops = [st[u, 0:1, rows] for u in range(UNITS)]
        tops3 = [st3[u, 0:1, rows3] for u in range(UNITS)]
        top = functools.reduce(jnp.maximum, tops)
        top_r = functools.reduce(jnp.maximum, tops3, top[:, 128:])
        top = jnp.concatenate([top[:, :128], top_r], 1)
        part = [jnp.exp2((t - top) * C2) for t in tops]
        part3 = [jnp.exp2((t - top_r) * C2) for t in tops3]
        total = sum(st[u, 1:2, rows] * part[u] for u in range(UNITS))
        total3 = sum(st3[u, 1:2, rows3] * part3[u] for u in range(UNITS))
        rdot = sum(st[u, 2:3, rows] * part[u] for u in range(UNITS))
        rdot3 = sum(st3[u, 2:3, rows3] * part3[u] for u in range(UNITS))
        inv = 1.0 / (total + jnp.concatenate([zero, total3], 1))
        rdot = (rdot + jnp.concatenate([zero, rdot3], 1)) * inv
        wrow[0:1, rows] = rdot
        for u in range(UNITS):
            st[u, 0:1, rows] = part[u] * inv
            st3[u, 0:1, rows3] = part3[u] * inv[:, 128:]

    def grad_scores(u):
        @pl.loop(0, HEADS, unroll=True)
        def _(h):
            at = pl.multiple_of(h * 256, 256)
            rows = pl.ds(at, 256)
            rows3 = pl.ds(pl.multiple_of(h * 128, 128), 128)
            rdot = wrow[0:1, rows]
            pr = prob[u, :, rows] * st[u, 0:1, rows]
            pb[u, :, rows] = pr.astype(BF16)
            dsb[pl.ds(256 * u, 256), rows] = (pr * (gprob[u, :, rows] - rdot)).astype(BF16)
            pr3 = prob3[u, :, rows3] * st3[u, 0:1, rows3]
            p3b[u, :, rows3] = pr3.astype(BF16)
            ds3b[pl.ds(128 * u, 128), rows3] = (
                pr3 * (gprob3[u, :, rows3] - rdot[:, 128:])
            ).astype(BF16)

    def grad_kv(u):
        dv = dot(pb[u], docat[...])
        dv3 = dot(p3b[u], bdo3[...])
        dk = dot(dsb[pl.ds(256 * u, 256), :], qcat[...]) * SCALE
        dk3 = dot(ds3b[pl.ds(128 * u, 128), :], bq3[...]) * SCALE
        for b in range(4):
            for col, big, small in ((0, dk, dk3), (128, dv, dv3)):
                cols = pl.ds(col, 128)
                stage[u, b, 0:64, cols] = big[64 * b : 64 * b + 64].astype(BF16)
                stage[u, b, 64:96, cols] = small[32 * b : 32 * b + 32, :128].astype(BF16)
                stage[u, b, 96:128, cols] = small[32 * b : 32 * b + 32, 128:].astype(BF16)

    back = []

    def part(m):
        return stage.at[m // 4, xor(s, m) % 4]

    def give(m, slot, to):
        cp = remote(part(m), rs.at[slot], rs_send.at[slot], rs_recv.at[slot], seq_dev(to))
        cp.start()
        back.append(cp)

    def landed(slot):
        remote(
            rs.at[slot], rs.at[slot], rs_send.at[slot], rs_recv.at[slot], seq_dev(1)
        ).wait_recv()

    def add(m, *slots):
        total = part(m)[...].astype(F32)
        for slot in slots:
            landed(slot)
            total = total + rs[slot].astype(F32)
        part(m)[...] = total.astype(BF16)

    def grad_queries():
        lane = lax.broadcasted_iota(jnp.int32, (128, 128), 1)
        for h in range(HEADS):
            rows = pl.ds(h * 256, 256)
            rows3 = pl.ds(h * 128, 128)
            dqt = dot(kt[...], dsb[:, rows])
            dqt3 = dot(kt3[...], ds3b[:, rows3])
            right = dqt[:, 128:] + jnp.where(lane < 64, dqt3[:128], dqt3[128:])
            left = dqt[:, :128].T * SCALE
            right = right.T * SCALE
            vec[h : h + 1, :] = jnp.sum(left + right, 0, keepdims=True)
            cols = pl.ds(h * DIM, DIM)
            for blk in range(2):
                dqst[blk, 0:64, cols] = left[64 * blk : 64 * blk + 64]
                dqst[blk, 64:96, cols] = right[32 * blk : 32 * blk + 32]
                dqst[blk, 96:128, cols] = right[64 + 32 * blk : 96 + 32 * blk]

    grad_scores(3)
    grad_kv(3)
    give(12, 0, 8)
    give(14, 2, 6)
    give(13, 1, 8)
    give(15, 3, 6)
    for u in (2, 1, 0):
        grad_scores(u)
    grad_queries()
    vec[7:8, :] = dot(jnp.ones((8, LANES), BF16), docat[...])[0:1]
    sums = []
    for k in range(8):
        sums.append(
            remote(
                vec,
                ar1.at[k, core],
                a_send.at[k],
                a_recv.at[2 * k + core],
                {"seq": xor(s, 2 * k) + 1 - core, "pair": p},
            )
        )
    for k in range(1, 8):
        sums[k].start()

    @pl.when(core == 0)
    def _():
        sums[0].start()

    def pair_step(group, buf, at):
        return [
            remote(buf.at[0], buf.at[k + 1], a_send.at[at + k], b_recv.at[at + k], pair_dev(n))
            for k, n in enumerate(group)
        ]

    near_step, far_step = pair_step(near, ar2, 8), pair_step(far, ar3, 11)
    last = remote(res, res, a_send.at[18], b_recv.at[18], seq_dev(1))

    grad_kv(2)
    give(10, 4, 2)
    give(11, 5, 2)
    grad_kv(1)
    give(6, 6, 6)

    @pl.when(core == 1)
    def _():
        total = [None, vec[...]]
        for k in range(8):
            for c in range(2):
                if (k, c) == (0, 1):
                    continue
                remote(
                    vec, ar1.at[k, c], a_send.at[k], a_recv.at[2 * k + c], seq_dev(1)
                ).wait_recv()
                total[c] = ar1[k, c] if total[c] is None else total[c] + ar1[k, c]
        ar2[0, 0] = total[0]
        ar2[0, 1] = total[1]
        if near:
            pl.semaphore_wait(barrier, len(near) + len(far))
        for cp in near_step:
            cp.start()

    dq_far = remote(
        dqst.at[other], dq_hbm.at[:, own_cols], dq_sem.at[0], dq_sem.at[1], seq_dev(1)
    )
    dq_far.start()
    dq_own = pltpu.make_async_copy(dqst.at[core], dq_hbm.at[:, own_cols], dq_sem.at[2])
    dq_own.start()
    add(4, 0)
    give(4, 7, 6)
    add(5, 1)
    give(5, 8, 2)
    grad_kv(0)
    give(3, 9, 3)
    give(1, 10, 1)

    @pl.when(core == 1)
    def _():
        total = ar2[0]
        for k, cp in enumerate(near_step):
            cp.wait_recv()
            total = total + ar2[k + 1]
        ar3[0] = total
        for cp in far_step:
            cp.start()

    add(8, 2, 4)
    give(8, 11, 8)
    add(9, 3, 5)
    give(9, 12, 9)
    add(2, 7)
    give(2, 13, 2)
    add(7, 8)
    give(7, 14, 7)

    @pl.when(core == 1)
    def _():
        total = ar3[0]
        for k, cp in enumerate(far_step):
            cp.wait_recv()
            total = total + ar3[k + 1]
        res[...] = total
        last.start()

    mine = part(0)[...].astype(F32)
    for slot in (6, 11, 13):
        landed(slot)
        mine = mine + rs[slot].astype(F32)
    theirs = jnp.zeros((128, 256), F32)
    for slot in (10, 9, 12, 14):
        landed(slot)
        theirs = theirs + rs[slot].astype(F32)
    for head, value in ((core, mine), (other, theirs)):
        dkv_ref[:, pl.ds(pl.multiple_of(head * 128, 128), 128)] = value[:, :128]
        dkv_ref[:, pl.ds(pl.multiple_of(256 + head * 128, 128), 128)] = value[:, 128:]

    @pl.when(core == 0)
    def _():
        last.wait_recv()

    for head in range(2):
        for h in range(HEADS):
            bq_ref[pl.ds((head * HEADS + h) * DIM, DIM)] = res[head, h]
        bv_ref[pl.ds(head * DIM, DIM)] = res[head, 7]

    dq_own.wait()
    dq_far.wait_recv()
    dq_far.wait_send()
    qx.wait_send()
    dx.wait_send()
    for cp in list(pushes.values()) + back + sums[1:]:
        cp.wait_send()

    @pl.when(core == 0)
    def _():
        sums[0].wait_send()

    @pl.when(core == 1)
    def _():
        for cp in near_step + far_step + [last]:
            cp.wait_send()


def hand_out(*refs):
    ins, outs, sem = refs[:4], refs[4:8], refs[8]
    copies = [pltpu.make_async_copy(a, b, sem.at[i]) for i, (a, b) in enumerate(zip(ins, outs))]
    for cp in copies:
        cp.start()
    for cp in copies:
        cp.wait()


def on_device(pairs, queries, keys_values, cotangent, resp_len, query_bias):
    near = [n for n in range(1, min(pairs, 4))]
    far = [n for n in range(4, pairs, 4)]
    vm = pltpu.VMEM
    dma = pltpu.SemaphoreType.DMA
    any_spec = pl.BlockSpec(memory_space=pl.ANY)
    hbm_spec = pl.BlockSpec(memory_space=pltpu.HBM)
    vmem_spec = pl.BlockSpec(memory_space=pltpu.VMEM)
    scratch = [
        vm((2, 2, 128, 128), BF16),
        vm((16, 2, 128, 128), BF16),
        vm((2, 128, RLANES), BF16),
        vm((2, 128, RLANES), BF16),
        vm((LANES, 128), BF16),
        vm((LANES, 128), BF16),
        vm((RLANES, 256), BF16),
        vm((RLANES, 256), BF16),
        vm((UNITS, 256, 128), BF16),
        vm((UNITS, 256, 128), BF16),
        vm((UNITS, 128, 256), BF16),
        vm((UNITS, 128, 256), BF16),
        vm((128, UNITS * 256), BF16),
        vm((256, UNITS * 128), BF16),
        vm((256, 128), F32),
        vm((UNITS, 128, 128), F32),
        vm((UNITS, 256, LANES), F32),
        vm((UNITS, 256, LANES), F32),
        vm((UNITS, 128, RLANES), F32),
        vm((UNITS, 128, RLANES), F32),
        vm((UNITS, 8, LANES), F32),
        vm((UNITS, 8, RLANES), F32),
        vm((8, LANES), F32),
        vm((UNITS, 256, LANES), BF16),
        vm((UNITS * 256, LANES), BF16),
        vm((UNITS, 128, RLANES), BF16),
        vm((UNITS * 128, RLANES), BF16),
        vm((UNITS, 4, 128, 256), BF16),
        vm((16, 128, 256), BF16),
        vm((2, 128, RLANES), F32),
        vm((8, 128), F32),
        vm((8, 2, 8, 128), F32),
        vm((len(near) + 1, 2, 8, 128), F32),
        vm((len(far) + 1, 2, 8, 128), F32),
        vm((2, 8, 128), F32),
        pltpu.SMEM((1, 2), jnp.int32),
        vm((2 * RLANES,), F32),
        dma((8,)),
        dma((16,)),
        dma((16,)),
        dma((2,)),
        dma((2,)),
        dma((16,)),
        dma((16,)),
        dma((3,)),
        dma((19,)),
        dma((16,)),
        dma((19,)),
        pltpu.SemaphoreType.REGULAR,
    ]
    shapes = (
        jax.ShapeDtypeStruct((128, 2 * RLANES), F32),
        jax.ShapeDtypeStruct((128, 512), F32),
        jax.ShapeDtypeStruct((2 * RLANES,), F32),
        jax.ShapeDtypeStruct((256,), F32),
    )
    made = pl.pallas_call(
        functools.partial(kernel, near, far),
        out_shape=shapes,
        in_specs=[
            hbm_spec,
            hbm_spec,
            hbm_spec,
            hbm_spec,
            hbm_spec,
        ],
        out_specs=(any_spec, vmem_spec, vmem_spec, vmem_spec),
        scratch_shapes=scratch,
        compiler_params=pltpu.CompilerParams(
            collective_id=0, has_side_effects=True, vmem_limit_bytes=63 * 1024 * 1024
        ),
    )(queries[0], keys_values[0], cotangent[0], resp_len, query_bias)
    dq, dkv, bq, bv = pl.pallas_call(
        hand_out,
        out_shape=shapes,
        in_specs=[vmem_spec] * 4,
        out_specs=(any_spec,) * 4,
        scratch_shapes=[dma((4,))],
    )(*made)
    return dq[None], dkv[None], bq, bv


def solution(mesh):
    return jax.shard_map(
        functools.partial(on_device, mesh.shape["pair"]),
        mesh=mesh,
        in_specs=(
            P("pair", "seq", None),
            P("pair", "seq", None),
            P("pair", "seq", None),
            P("pair", None),
            P(),
        ),
        out_specs=(P("pair", "seq", None), P("pair", "seq", None), P(), P()),
        check_vma=False,
    )
```

```python
import functools
import math

import jax
import jax.numpy as jnp
from jax import lax
from jax.experimental import pallas as pl
from jax.experimental.pallas import tpu as pltpu
from jax.sharding import PartitionSpec as P

HEADS = 7
DIM = 128
ROWS = 128
LANES = HEADS * 2 * ROWS
RLANES = HEADS * ROWS
UNITS = 4
SCALE = 1.0 / math.sqrt(DIM)
C2 = SCALE * math.log2(math.e)
NEG = -1e30
MESH = pl.DeviceIdType.MESH
F32, BF16 = jnp.float32, jnp.bfloat16


def xor(value, mask):
    out = value
    bit = 1
    while bit <= mask:
        if mask & bit:
            out = out + bit - 2 * bit * ((value // bit) % 2)
        bit *= 2
    return out


def dot_nt(a, b):
    return lax.dot_general(a, b, (((1,), (1,)), ((), ())), preferred_element_type=F32)


def dot(a, b):
    return jnp.dot(a, b, preferred_element_type=F32)


def kernel(
    pairs,
    q_hbm,
    kv_hbm,
    cot_hbm,
    len_hbm,
    bias_hbm,
    dq_hbm,
    dkv_ref,
    bq_ref,
    bv_ref,
    kvs,
    kvg,
    qin,
    doin,
    qcat,
    docat,
    bq3,
    bdo3,
    kp,
    vp,
    k3,
    v3,
    kt,
    kt3,
    bias12,
    bias3,
    prob,
    gprob,
    prob3,
    gprob3,
    st,
    st3,
    wrow,
    pb,
    dsb,
    p3b,
    ds3b,
    stage,
    rs,
    dqst,
    vec,
    ar1,
    ar2,
    res,
    len_ref,
    bias_ref,
    loc_sem,
    kv_send,
    kv_recv,
    x_send,
    x_recv,
    rs_send,
    rs_recv,
    dq_sem,
    a_send,
    a_recv,
    b_send,
    b_recv,
    c_send,
    c_recv,
    go_sem,
):
    s = lax.axis_index("seq")
    p = lax.axis_index("pair")
    chip = s // 2
    core = s % 2
    other = 1 - core
    duo = s // 4

    def seq_dev(m):
        return {"seq": xor(s, m), "pair": p}

    def pair_dev(n):
        return {"seq": s, "pair": xor(p, n)}

    own_cols = pl.ds(pl.multiple_of(core * RLANES, 128), RLANES)
    other_cols = pl.ds(pl.multiple_of(other * RLANES, 128), RLANES)

    local = []
    for h in range(2):
        for part in range(2):
            local.append(
                pltpu.make_async_copy(
                    kv_hbm.at[:, pl.ds((2 * part + h) * DIM, DIM)],
                    kvs.at[h, part],
                    loc_sem.at[2 * h + part],
                )
            )
    local.append(pltpu.make_async_copy(q_hbm.at[:, own_cols], qin.at[core], loc_sem.at[4]))
    local.append(pltpu.make_async_copy(cot_hbm.at[:, own_cols], doin.at[core], loc_sem.at[5]))
    local.append(pltpu.make_async_copy(bias_hbm, bias_ref, loc_sem.at[6]))
    local.append(pltpu.make_async_copy(len_hbm, len_ref, loc_sem.at[7]))
    for cp in local:
        cp.start()

    barrier = pltpu.get_barrier_semaphore()

    @pl.when(core == 0)
    def _():
        for m in (2, 6, 8):
            pl.semaphore_signal(barrier, inc=1, device_id=seq_dev(m), device_id_type=MESH)

    @pl.when(core == 1)
    def _():
        for m in (3, 7, 9, 1):
            pl.semaphore_signal(barrier, inc=1, device_id=seq_dev(m), device_id_type=MESH)

    for cp in local[:4]:
        cp.wait()

    @pl.when(core == 0)
    def _():
        pl.semaphore_wait(barrier, 7)
        pl.semaphore_signal(go_sem, inc=1, device_id=seq_dev(1), device_id_type=MESH)

    @pl.when(core == 1)
    def _():
        pl.semaphore_wait(go_sem, 1)

    def remote(src, dst, send, recv, dev):
        return pltpu.make_async_remote_copy(
            src_ref=src,
            dst_ref=dst,
            send_sem=send,
            recv_sem=recv,
            device_id=dev,
            device_id_type=MESH,
        )

    pushes = {}

    def push(src, block, mask, to):
        cp = remote(src, kvg.at[block], kv_send.at[mask], kv_recv.at[mask], seq_dev(to))
        cp.start()
        pushes[mask] = cp

    for m in (2, 7, 8, 3, 6, 9, 1):
        push(kvs.at[xor(s, m) % 2], s, m, m)
    qx = remote(q_hbm.at[:, other_cols], qin.at[core], x_send.at[0], x_recv.at[0], seq_dev(1))
    dx = remote(cot_hbm.at[:, other_cols], doin.at[core], x_send.at[1], x_recv.at[1], seq_dev(1))
    qx.start()
    dx.start()

    @pl.when(core == 1)
    def _():
        for n in range(1, pairs):
            pl.semaphore_signal(barrier, inc=1, device_id=pair_dev(n), device_id_type=MESH)

    kvg[s] = kvs[core]

    local[7].wait()
    len0, len1 = len_ref[0, 0], len_ref[0, 1]
    key = lax.broadcasted_iota(jnp.int32, (256, 128), 0)
    lane = lax.broadcasted_iota(jnp.int32, (256, 128), 1)
    bias12[...] = jnp.where(key + 256 * duo <= lane + 128 * chip, 0.0, NEG).astype(F32)
    key = lax.broadcasted_iota(jnp.int32, (128, 128), 0)
    lane = lax.broadcasted_iota(jnp.int32, (128, 128), 1)
    place_q = jnp.where(lane < 64, lane, lane - 64) + 64 * chip
    limit = jnp.where(lane < 64, len0, len1)
    for u in range(UNITS):
        place_k = key + 128 * xor(duo, u)
        seen = (place_k <= place_q) & (place_k < limit)
        bias3[u] = jnp.where(seen, 0.0, NEG).astype(F32)

    bq3[...] = jnp.zeros_like(bq3)
    bdo3[...] = jnp.zeros_like(bdo3)
    row = lax.broadcasted_iota(jnp.int32, (32, 128), 0)

    def prepare(blk):
        base = 32 * (2 * chip + blk)
        for h in range(HEADS):
            cols = pl.ds(h * DIM, DIM)
            bias = bias_ref[pl.ds(pl.multiple_of((core * HEADS + h) * DIM, 128), DIM)][None]
            x = (qin[blk, :, cols].astype(F32) + bias).astype(BF16)
            d = doin[blk, :, cols]
            d1 = jnp.where(row + base < len0, d[64:96].astype(F32), 0.0).astype(BF16)
            d2 = jnp.where(row + base < len1, d[96:128].astype(F32), 0.0).astype(BF16)
            for cat, block, y0, y1, y2 in (
                (qcat, bq3, x[0:64], x[64:96], x[96:128]),
                (docat, bdo3, d[0:64], d1, d2),
            ):
                at = h * 256
                cat[pl.ds(pl.multiple_of(at + 64 * blk, 64), 64), :] = y0
                cat[pl.ds(pl.multiple_of(at + 128 + 32 * blk, 32), 32), :] = y1
                cat[pl.ds(pl.multiple_of(at + 192 + 32 * blk, 32), 32), :] = y2
                block[pl.ds(pl.multiple_of(h * 128 + 32 * blk, 32), 32), pl.ds(0, 128)] = y1
                block[pl.ds(pl.multiple_of(h * 128 + 64 + 32 * blk, 32), 32), pl.ds(128, 128)] = y2

    def relay(held, *ways):
        pushes[held].wait_recv()
        for mask, to in ways:
            push(kvg.at[xor(s, held)], xor(s, held), mask, to)

    relay(2, (4, 6))
    relay(7, (5, 2))
    for k in (4, 5, 6):
        local[k].wait()
    prepare(core)
    relay(8, (10, 2), (14, 6))
    relay(9, (11, 2), (15, 6))
    qx.wait_recv()
    dx.wait_recv()
    prepare(other)
    more = {0: ((3,), (6,), (1,)), 1: ((4, (12, 8)), (5, (13, 8))), 2: ((10,), (11,))}
    more[3] = ((12,), (13,), (14,), (15,))

    def gather_unit(u):
        for way in more[u]:
            relay(*way)
        first = 4 * xor(duo, u)

        def rows(part, start, size):
            return jnp.concatenate(
                [kvg[first + b, part, pl.ds(start, size), :] for b in range(4)], 0
            )

        kp[u] = rows(0, 0, 64)
        vp[u] = rows(1, 0, 64)
        k3[u, :, 0:128] = rows(0, 64, 32)
        k3[u, :, 128:256] = rows(0, 96, 32)
        v3[u, :, 0:128] = rows(1, 64, 32)
        v3[u, :, 128:256] = rows(1, 96, 32)
        kt[:, pl.ds(256 * u, 256)] = kp[u].astype(F32).T.astype(BF16)
        kt3[:, pl.ds(128 * u, 128)] = k3[u].astype(F32).T.astype(BF16)

    def phase_a(u):
        gather_unit(u)
        earlier = xor(duo, u) < duo

        @pl.loop(0, HEADS, unroll=True)
        def _(h):
            at = pl.multiple_of(h * 256, 256)
            at3 = pl.multiple_of(h * 128, 128)
            rows = pl.ds(at, 256)
            rows3 = pl.ds(at3, 128)
            sc = dot_nt(kp[u], qcat[rows, :])
            if u == 0:
                sc = jnp.concatenate([sc[:, :128] + bias12[...], sc[:, 128:]], 1)
            top = jnp.max(sc, 0, keepdims=True)
            pr = jnp.exp2((sc - top) * C2)
            gp = dot_nt(vp[u], docat[rows, :])
            prob[u, :, rows] = pr
            gprob[u, :, rows] = gp
            if u:
                lane1 = lax.broadcasted_iota(jnp.int32, (1, 256), 1)
                top = jnp.where((lane1 >= 128) | earlier, top, NEG)
            st[u, 0:1, rows] = top
            st[u, 1:2, rows] = jnp.sum(pr, 0, keepdims=True)
            st[u, 2:3, rows] = jnp.sum(pr * gp, 0, keepdims=True)

            sc3 = dot_nt(k3[u], bq3[rows3, :]) + bias3[u]
            top3 = jnp.max(sc3, 0, keepdims=True)
            pr3 = jnp.exp2((sc3 - top3) * C2)
            gp3 = dot_nt(v3[u], bdo3[rows3, :])
            prob3[u, :, rows3] = pr3
            gprob3[u, :, rows3] = gp3
            st3[u, 0:1, rows3] = top3
            st3[u, 1:2, rows3] = jnp.sum(pr3, 0, keepdims=True)
            st3[u, 2:3, rows3] = jnp.sum(pr3 * gp3, 0, keepdims=True)

    for u in range(UNITS):
        phase_a(u)

    @pl.loop(0, HEADS)
    def _(h):
        rows = pl.ds(pl.multiple_of(h * 256, 256), 256)
        rows3 = pl.ds(pl.multiple_of(h * 128, 128), 128)
        zero = jnp.zeros((1, 128), F32)
        tops = [st[u, 0:1, rows] for u in range(UNITS)]
        tops3 = [st3[u, 0:1, rows3] for u in range(UNITS)]
        top = functools.reduce(jnp.maximum, tops)
        top_r = functools.reduce(jnp.maximum, tops3, top[:, 128:])
        top = jnp.concatenate([top[:, :128], top_r], 1)
        part = [jnp.exp2((t - top) * C2) for t in tops]
        part3 = [jnp.exp2((t - top_r) * C2) for t in tops3]
        total = sum(st[u, 1:2, rows] * part[u] for u in range(UNITS))
        total3 = sum(st3[u, 1:2, rows3] * part3[u] for u in range(UNITS))
        rdot = sum(st[u, 2:3, rows] * part[u] for u in range(UNITS))
        rdot3 = sum(st3[u, 2:3, rows3] * part3[u] for u in range(UNITS))
        inv = 1.0 / (total + jnp.concatenate([zero, total3], 1))
        rdot = (rdot + jnp.concatenate([zero, rdot3], 1)) * inv
        wrow[0:1, rows] = rdot
        for u in range(UNITS):
            st[u, 0:1, rows] = part[u] * inv
            st3[u, 0:1, rows3] = part3[u] * inv[:, 128:]

    def grad_scores(u):
        @pl.loop(0, HEADS, unroll=True)
        def _(h):
            at = pl.multiple_of(h * 256, 256)
            rows = pl.ds(at, 256)
            rows3 = pl.ds(pl.multiple_of(h * 128, 128), 128)
            rdot = wrow[0:1, rows]
            pr = prob[u, :, rows] * st[u, 0:1, rows]
            pb[u, :, rows] = pr.astype(BF16)
            dsb[pl.ds(256 * u, 256), rows] = (pr * (gprob[u, :, rows] - rdot)).astype(BF16)
            pr3 = prob3[u, :, rows3] * st3[u, 0:1, rows3]
            p3b[u, :, rows3] = pr3.astype(BF16)
            ds3b[pl.ds(128 * u, 128), rows3] = (
                pr3 * (gprob3[u, :, rows3] - rdot[:, 128:])
            ).astype(BF16)

    def grad_kv(u):
        dv = dot(pb[u], docat[...])
        dv3 = dot(p3b[u], bdo3[...])
        dk = dot(dsb[pl.ds(256 * u, 256), :], qcat[...]) * SCALE
        dk3 = dot(ds3b[pl.ds(128 * u, 128), :], bq3[...]) * SCALE
        for b in range(4):
            for col, big, small in ((0, dk, dk3), (128, dv, dv3)):
                cols = pl.ds(col, 128)
                stage[u, b, 0:64, cols] = big[64 * b : 64 * b + 64].astype(BF16)
                stage[u, b, 64:96, cols] = small[32 * b : 32 * b + 32, :128].astype(BF16)
                stage[u, b, 96:128, cols] = small[32 * b : 32 * b + 32, 128:].astype(BF16)

    back = []

    def part(m):
        return stage.at[m // 4, xor(s, m) % 4]

    def give(m, slot, to):
        cp = remote(part(m), rs.at[slot], rs_send.at[slot], rs_recv.at[slot], seq_dev(to))
        cp.start()
        back.append(cp)

    def landed(slot):
        remote(
            rs.at[slot], rs.at[slot], rs_send.at[slot], rs_recv.at[slot], seq_dev(1)
        ).wait_recv()

    def add(m, *slots):
        total = part(m)[...].astype(F32)
        for slot in slots:
            landed(slot)
            total = total + rs[slot].astype(F32)
        part(m)[...] = total.astype(BF16)

    def grad_queries():
        lane = lax.broadcasted_iota(jnp.int32, (128, 128), 1)
        for h in range(HEADS):
            rows = pl.ds(h * 256, 256)
            rows3 = pl.ds(h * 128, 128)
            dqt = dot(kt[...], dsb[:, rows])
            dqt3 = dot(kt3[...], ds3b[:, rows3])
            right = dqt[:, 128:] + jnp.where(lane < 64, dqt3[:128], dqt3[128:])
            left = dqt[:, :128].T * SCALE
            right = right.T * SCALE
            vec[h] = jnp.sum(left + right, 0, keepdims=True)
            cols = pl.ds(h * DIM, DIM)
            for blk in range(2):
                dqst[blk, 0:64, cols] = left[64 * blk : 64 * blk + 64]
                dqst[blk, 64:96, cols] = right[32 * blk : 32 * blk + 32]
                dqst[blk, 96:128, cols] = right[64 + 32 * blk : 96 + 32 * blk]

    grad_scores(3)
    grad_kv(3)
    give(12, 0, 8)
    give(14, 2, 6)
    give(13, 1, 8)
    give(15, 3, 6)
    for u in (2, 1, 0):
        grad_scores(u)
    grad_queries()
    vec[7] = dot(jnp.ones((8, LANES), BF16), docat[...])[0:1]
    sums = []
    for k in range(8):
        sums.append(
            remote(
                vec.at[xor(s, 2 * k) // 2],
                ar1.at[k, core],
                a_send.at[k],
                a_recv.at[2 * k + core],
                {"seq": xor(s, 2 * k) + 1 - core, "pair": p},
            )
        )
    for k in range(1, 8):
        sums[k].start()

    @pl.when(core == 0)
    def _():
        sums[0].start()

    pair_step = [
        remote(ar2.at[0], ar2.at[n], b_send.at[n], b_recv.at[n], pair_dev(n))
        for n in range(1, pairs)
    ]
    spread = [
        remote(res.at[chip], res.at[chip], c_send.at[m], c_recv.at[m // 2], seq_dev(m))
        for m in range(1, 16)
    ]

    grad_kv(2)
    give(10, 4, 2)
    give(11, 5, 2)

    grad_kv(1)
    give(6, 6, 6)

    @pl.when(core == 1)
    def _():
        total = [None, vec[chip]]
        for k in range(8):
            for c in range(2):
                if (k, c) == (0, 1):
                    continue
                remote(
                    ar1.at[k, c], ar1.at[k, c], a_send.at[k], a_recv.at[2 * k + c], seq_dev(1)
                ).wait_recv()
                total[c] = ar1[k, c] if total[c] is None else total[c] + ar1[k, c]
        ar2[0, 0:1] = total[0]
        ar2[0, 1:2] = total[1]
        if pairs > 1:
            pl.semaphore_wait(barrier, pairs - 1)
        for cp in pair_step:
            cp.start()


    dq_far = remote(
        dqst.at[other], dq_hbm.at[:, own_cols], dq_sem.at[0], dq_sem.at[1], seq_dev(1)
    )
    dq_far.start()
    dq_own = pltpu.make_async_copy(dqst.at[core], dq_hbm.at[:, own_cols], dq_sem.at[2])
    dq_own.start()
    add(4, 0)
    give(4, 7, 6)
    add(5, 1)
    give(5, 8, 2)
    grad_kv(0)
    give(3, 9, 3)
    give(1, 10, 1)

    add(8, 2, 4)
    give(8, 11, 8)
    add(9, 3, 5)
    give(9, 12, 9)
    add(2, 7)
    give(2, 13, 2)
    add(7, 8)
    give(7, 14, 7)

    @pl.when(core == 1)
    def _():
        total = ar2[0]
        for n in range(1, pairs):
            pair_step[n - 1].wait_recv()
            total = total + ar2[n]
        res[chip] = total
        for cp in spread:
            cp.start()

    mine = part(0)[...].astype(F32)
    for slot in (6, 11, 13):
        landed(slot)
        mine = mine + rs[slot].astype(F32)
    theirs = jnp.zeros((128, 256), F32)
    for slot in (10, 9, 12, 14):
        landed(slot)
        theirs = theirs + rs[slot].astype(F32)
    for head, value in ((core, mine), (other, theirs)):
        dkv_ref[:, pl.ds(pl.multiple_of(head * 128, 128), 128)] = value[:, :128]
        dkv_ref[:, pl.ds(pl.multiple_of(256 + head * 128, 128), 128)] = value[:, 128:]

    def rows_from(k):
        at = res.at[xor(s, 2 * k) // 2]
        remote(at, at, c_send.at[k], c_recv.at[k], seq_dev(1)).wait_recv()

    @pl.when(core == 0)
    def _():
        rows_from(0)

    for k in range(1, 8):
        rows_from(k)
    for head in range(2):
        for h in range(HEADS):
            bq_ref[pl.ds((head * HEADS + h) * DIM, DIM)] = res[h, head]
        bv_ref[pl.ds(head * DIM, DIM)] = res[7, head]

    dq_own.wait()
    dq_far.wait_recv()
    dq_far.wait_send()
    qx.wait_send()
    dx.wait_send()
    for cp in list(pushes.values()) + back + sums[1:]:
        cp.wait_send()

    @pl.when(core == 0)
    def _():
        sums[0].wait_send()

    @pl.when(core == 1)
    def _():
        for cp in pair_step + spread:
            cp.wait_send()


def hand_out(*refs):
    ins, outs, sem = refs[:4], refs[4:8], refs[8]
    copies = [pltpu.make_async_copy(a, b, sem.at[i]) for i, (a, b) in enumerate(zip(ins, outs))]
    for cp in copies:
        cp.start()
    for cp in copies:
        cp.wait()


def on_device(pairs, queries, keys_values, cotangent, resp_len, query_bias):
    vm = pltpu.VMEM
    dma = pltpu.SemaphoreType.DMA
    any_spec = pl.BlockSpec(memory_space=pl.ANY)
    hbm_spec = pl.BlockSpec(memory_space=pltpu.HBM)
    vmem_spec = pl.BlockSpec(memory_space=pltpu.VMEM)
    scratch = [
        vm((2, 2, 128, 128), BF16),
        vm((16, 2, 128, 128), BF16),
        vm((2, 128, RLANES), BF16),
        vm((2, 128, RLANES), BF16),
        vm((LANES, 128), BF16),
        vm((LANES, 128), BF16),
        vm((RLANES, 256), BF16),
        vm((RLANES, 256), BF16),
        vm((UNITS, 256, 128), BF16),
        vm((UNITS, 256, 128), BF16),
        vm((UNITS, 128, 256), BF16),
        vm((UNITS, 128, 256), BF16),
        vm((128, UNITS * 256), BF16),
        vm((256, UNITS * 128), BF16),
        vm((256, 128), F32),
        vm((UNITS, 128, 128), F32),
        vm((UNITS, 256, LANES), F32),
        vm((UNITS, 256, LANES), F32),
        vm((UNITS, 128, RLANES), F32),
        vm((UNITS, 128, RLANES), F32),
        vm((UNITS, 8, LANES), F32),
        vm((UNITS, 8, RLANES), F32),
        vm((8, LANES), F32),
        vm((UNITS, 256, LANES), BF16),
        vm((UNITS * 256, LANES), BF16),
        vm((UNITS, 128, RLANES), BF16),
        vm((UNITS * 128, RLANES), BF16),
        vm((UNITS, 4, 128, 256), BF16),
        vm((16, 128, 256), BF16),
        vm((2, 128, RLANES), F32),
        vm((8, 1, 128), F32),
        vm((8, 2, 1, 128), F32),
        vm((pairs, 2, 128), F32),
        vm((8, 2, 128), F32),
        pltpu.SMEM((1, 2), jnp.int32),
        vm((2 * RLANES,), F32),
        dma((8,)),
        dma((16,)),
        dma((16,)),
        dma((2,)),
        dma((2,)),
        dma((16,)),
        dma((16,)),
        dma((3,)),
        dma((8,)),
        dma((16,)),
        dma((pairs,)),
        dma((pairs,)),
        dma((16,)),
        dma((8,)),
        pltpu.SemaphoreType.REGULAR,
    ]
    shapes = (
        jax.ShapeDtypeStruct((128, 2 * RLANES), F32),
        jax.ShapeDtypeStruct((128, 512), F32),
        jax.ShapeDtypeStruct((2 * RLANES,), F32),
        jax.ShapeDtypeStruct((256,), F32),
    )
    made = pl.pallas_call(
        functools.partial(kernel, pairs),
        out_shape=shapes,
        in_specs=[
            hbm_spec,
            hbm_spec,
            hbm_spec,
            hbm_spec,
            hbm_spec,
        ],
        out_specs=(any_spec, vmem_spec, vmem_spec, vmem_spec),
        scratch_shapes=scratch,
        compiler_params=pltpu.CompilerParams(
            collective_id=0, has_side_effects=True, vmem_limit_bytes=63 * 1024 * 1024
        ),
    )(queries[0], keys_values[0], cotangent[0], resp_len, query_bias)
    dq, dkv, bq, bv = pl.pallas_call(
        hand_out,
        out_shape=shapes,
        in_specs=[vmem_spec] * 4,
        out_specs=(any_spec,) * 4,
        scratch_shapes=[dma((4,))],
    )(*made)
    return dq[None], dkv[None], bq, bv


def solution(mesh):
    return jax.shard_map(
        functools.partial(on_device, mesh.shape["pair"]),
        mesh=mesh,
        in_specs=(
            P("pair", "seq", None),
            P("pair", "seq", None),
            P("pair", "seq", None),
            P("pair", None),
            P(),
        ),
        out_specs=(P("pair", "seq", None), P("pair", "seq", None), P(), P()),
        check_vma=False,
    )
```

```python
import functools
import math

import jax
import jax.numpy as jnp
from jax import lax
from jax.experimental import pallas as pl
from jax.experimental.pallas import tpu as pltpu
from jax.sharding import PartitionSpec as P

HEADS = 7
DIM = 128
ROWS = 128
LANES = HEADS * 2 * ROWS
RLANES = HEADS * ROWS
UNITS = 4
SCALE = 1.0 / math.sqrt(DIM)
C2 = SCALE * math.log2(math.e)
NEG = -1e30
MESH = pl.DeviceIdType.MESH
F32, BF16 = jnp.float32, jnp.bfloat16


def xor(value, mask):
    out = value
    bit = 1
    while bit <= mask:
        if mask & bit:
            out = out + bit - 2 * bit * ((value // bit) % 2)
        bit *= 2
    return out


def dot_nt(a, b):
    return lax.dot_general(a, b, (((1,), (1,)), ((), ())), preferred_element_type=F32)


def dot(a, b):
    return jnp.dot(a, b, preferred_element_type=F32)


def kernel(
    pairs,
    q_hbm,
    kv_hbm,
    cot_hbm,
    len_hbm,
    bias_hbm,
    dq_hbm,
    dkv_ref,
    bq_ref,
    bv_ref,
    kvs,
    kvg,
    qin,
    doin,
    qcat,
    docat,
    bq3,
    bdo3,
    kp,
    vp,
    k3,
    v3,
    kt,
    kt3,
    bias12,
    bias3,
    prob,
    gprob,
    prob3,
    gprob3,
    st,
    st3,
    wrow,
    pb,
    dsb,
    p3b,
    ds3b,
    stage,
    rs,
    dqst,
    vec,
    ar1,
    ar2,
    res,
    len_ref,
    bias_ref,
    loc_sem,
    kv_send,
    kv_recv,
    x_send,
    x_recv,
    rs_send,
    rs_recv,
    dq_sem,
    a_send,
    a_recv,
    b_send,
    b_recv,
    c_send,
    c_recv,
    go_sem,
):
    s = lax.axis_index("seq")
    p = lax.axis_index("pair")
    chip = s // 2
    core = s % 2
    other = 1 - core
    duo = s // 4

    def seq_dev(m):
        return {"seq": xor(s, m), "pair": p}

    def pair_dev(n):
        return {"seq": s, "pair": xor(p, n)}

    own_cols = pl.ds(pl.multiple_of(core * RLANES, 128), RLANES)
    other_cols = pl.ds(pl.multiple_of(other * RLANES, 128), RLANES)

    local = []
    for h in range(2):
        for part in range(2):
            local.append(
                pltpu.make_async_copy(
                    kv_hbm.at[:, pl.ds((2 * part + h) * DIM, DIM)],
                    kvs.at[h, part],
                    loc_sem.at[2 * h + part],
                )
            )
    local.append(pltpu.make_async_copy(q_hbm.at[:, own_cols], qin.at[core], loc_sem.at[4]))
    local.append(pltpu.make_async_copy(cot_hbm.at[:, own_cols], doin.at[core], loc_sem.at[5]))
    local.append(pltpu.make_async_copy(bias_hbm, bias_ref, loc_sem.at[6]))
    local.append(pltpu.make_async_copy(len_hbm, len_ref, loc_sem.at[7]))
    for cp in local:
        cp.start()

    barrier = pltpu.get_barrier_semaphore()

    @pl.when(core == 0)
    def _():
        for m in (2, 6, 8):
            pl.semaphore_signal(barrier, inc=1, device_id=seq_dev(m), device_id_type=MESH)

    @pl.when(core == 1)
    def _():
        for m in (3, 7, 9, 1):
            pl.semaphore_signal(barrier, inc=1, device_id=seq_dev(m), device_id_type=MESH)

    for cp in local[:4]:
        cp.wait()

    @pl.when(core == 0)
    def _():
        pl.semaphore_wait(barrier, 7)
        pl.semaphore_signal(go_sem, inc=1, device_id=seq_dev(1), device_id_type=MESH)

    @pl.when(core == 1)
    def _():
        pl.semaphore_wait(go_sem, 1)

    def remote(src, dst, send, recv, dev):
        return pltpu.make_async_remote_copy(
            src_ref=src,
            dst_ref=dst,
            send_sem=send,
            recv_sem=recv,
            device_id=dev,
            device_id_type=MESH,
        )

    pushes = {}

    def push(src, block, mask, to):
        cp = remote(src, kvg.at[block], kv_send.at[mask], kv_recv.at[mask], seq_dev(to))
        cp.start()
        pushes[mask] = cp

    for m in (2, 7, 8, 3, 6, 9, 1):
        push(kvs.at[xor(s, m) % 2], s, m, m)
    qx = remote(q_hbm.at[:, other_cols], qin.at[core], x_send.at[0], x_recv.at[0], seq_dev(1))
    dx = remote(cot_hbm.at[:, other_cols], doin.at[core], x_send.at[1], x_recv.at[1], seq_dev(1))
    qx.start()
    dx.start()

    @pl.when(core == 1)
    def _():
        for n in range(1, pairs):
            pl.semaphore_signal(barrier, inc=1, device_id=pair_dev(n), device_id_type=MESH)

    kvg[s] = kvs[core]

    local[7].wait()
    len0, len1 = len_ref[0, 0], len_ref[0, 1]
    key = lax.broadcasted_iota(jnp.int32, (256, 128), 0)
    lane = lax.broadcasted_iota(jnp.int32, (256, 128), 1)
    bias12[...] = jnp.where(key + 256 * duo <= lane + 128 * chip, 0.0, NEG).astype(F32)
    key = lax.broadcasted_iota(jnp.int32, (128, 128), 0)
    lane = lax.broadcasted_iota(jnp.int32, (128, 128), 1)
    place_q = jnp.where(lane < 64, lane, lane - 64) + 64 * chip
    limit = jnp.where(lane < 64, len0, len1)
    for u in range(UNITS):
        place_k = key + 128 * xor(duo, u)
        seen = (place_k <= place_q) & (place_k < limit)
        bias3[u] = jnp.where(seen, 0.0, NEG).astype(F32)

    bq3[...] = jnp.zeros_like(bq3)
    bdo3[...] = jnp.zeros_like(bdo3)
    row = lax.broadcasted_iota(jnp.int32, (32, 128), 0)

    def prepare(blk):
        base = 32 * (2 * chip + blk)
        for h in range(HEADS):
            cols = pl.ds(h * DIM, DIM)
            bias = bias_ref[pl.ds(pl.multiple_of((core * HEADS + h) * DIM, 128), DIM)][None]
            x = (qin[blk, :, cols].astype(F32) + bias).astype(BF16)
            d = doin[blk, :, cols]
            d1 = jnp.where(row + base < len0, d[64:96].astype(F32), 0.0).astype(BF16)
            d2 = jnp.where(row + base < len1, d[96:128].astype(F32), 0.0).astype(BF16)
            for cat, block, y0, y1, y2 in (
                (qcat, bq3, x[0:64], x[64:96], x[96:128]),
                (docat, bdo3, d[0:64], d1, d2),
            ):
                at = h * 256
                cat[pl.ds(pl.multiple_of(at + 64 * blk, 64), 64), :] = y0
                cat[pl.ds(pl.multiple_of(at + 128 + 32 * blk, 32), 32), :] = y1
                cat[pl.ds(pl.multiple_of(at + 192 + 32 * blk, 32), 32), :] = y2
                block[pl.ds(pl.multiple_of(h * 128 + 32 * blk, 32), 32), pl.ds(0, 128)] = y1
                block[pl.ds(pl.multiple_of(h * 128 + 64 + 32 * blk, 32), 32), pl.ds(128, 128)] = y2

    def relay(held, *ways):
        pushes[held].wait_recv()
        for mask, to in ways:
            push(kvg.at[xor(s, held)], xor(s, held), mask, to)

    relay(2, (4, 6))
    relay(7, (5, 2))
    for k in (4, 5, 6):
        local[k].wait()
    prepare(core)
    relay(8, (10, 2), (14, 6))
    relay(9, (11, 2), (15, 6))
    qx.wait_recv()
    dx.wait_recv()
    prepare(other)
    more = {0: ((3,), (6,), (1,)), 1: ((4, (12, 8)), (5, (13, 8))), 2: ((10,), (11,))}
    more[3] = ((12,), (13,), (14,), (15,))

    def gather_unit(u):
        for way in more[u]:
            relay(*way)
        first = 4 * xor(duo, u)

        def rows(part, start, size):
            return jnp.concatenate(
                [kvg[first + b, part, pl.ds(start, size), :] for b in range(4)], 0
            )

        kp[u] = rows(0, 0, 64)
        vp[u] = rows(1, 0, 64)
        k3[u, :, 0:128] = rows(0, 64, 32)
        k3[u, :, 128:256] = rows(0, 96, 32)
        v3[u, :, 0:128] = rows(1, 64, 32)
        v3[u, :, 128:256] = rows(1, 96, 32)
        kt[:, pl.ds(256 * u, 256)] = kp[u].astype(F32).T.astype(BF16)
        kt3[:, pl.ds(128 * u, 128)] = k3[u].astype(F32).T.astype(BF16)

    def phase_a(u):
        gather_unit(u)
        earlier = xor(duo, u) < duo

        @pl.loop(0, HEADS, unroll=True)
        def _(h):
            at = pl.multiple_of(h * 256, 256)
            at3 = pl.multiple_of(h * 128, 128)
            rows = pl.ds(at, 256)
            rows3 = pl.ds(at3, 128)
            sc = dot_nt(kp[u], qcat[rows, :])
            if u == 0:
                sc = jnp.concatenate([sc[:, :128] + bias12[...], sc[:, 128:]], 1)
            top = jnp.max(sc, 0, keepdims=True)
            pr = jnp.exp2((sc - top) * C2)
            gp = dot_nt(vp[u], docat[rows, :])
            prob[u, :, rows] = pr
            gprob[u, :, rows] = gp
            if u:
                lane1 = lax.broadcasted_iota(jnp.int32, (1, 256), 1)
                top = jnp.where((lane1 >= 128) | earlier, top, NEG)
            st[u, 0:1, rows] = top
            st[u, 1:2, rows] = jnp.sum(pr, 0, keepdims=True)
            st[u, 2:3, rows] = jnp.sum(pr * gp, 0, keepdims=True)

            sc3 = dot_nt(k3[u], bq3[rows3, :]) + bias3[u]
            top3 = jnp.max(sc3, 0, keepdims=True)
            pr3 = jnp.exp2((sc3 - top3) * C2)
            gp3 = dot_nt(v3[u], bdo3[rows3, :])
            prob3[u, :, rows3] = pr3
            gprob3[u, :, rows3] = gp3
            st3[u, 0:1, rows3] = top3
            st3[u, 1:2, rows3] = jnp.sum(pr3, 0, keepdims=True)
            st3[u, 2:3, rows3] = jnp.sum(pr3 * gp3, 0, keepdims=True)

    for u in range(UNITS):
        phase_a(u)

    @pl.loop(0, HEADS)
    def _(h):
        rows = pl.ds(pl.multiple_of(h * 256, 256), 256)
        rows3 = pl.ds(pl.multiple_of(h * 128, 128), 128)
        zero = jnp.zeros((1, 128), F32)
        tops = [st[u, 0:1, rows] for u in range(UNITS)]
        tops3 = [st3[u, 0:1, rows3] for u in range(UNITS)]
        top = functools.reduce(jnp.maximum, tops)
        top_r = functools.reduce(jnp.maximum, tops3, top[:, 128:])
        top = jnp.concatenate([top[:, :128], top_r], 1)
        part = [jnp.exp2((t - top) * C2) for t in tops]
        part3 = [jnp.exp2((t - top_r) * C2) for t in tops3]
        total = sum(st[u, 1:2, rows] * part[u] for u in range(UNITS))
        total3 = sum(st3[u, 1:2, rows3] * part3[u] for u in range(UNITS))
        rdot = sum(st[u, 2:3, rows] * part[u] for u in range(UNITS))
        rdot3 = sum(st3[u, 2:3, rows3] * part3[u] for u in range(UNITS))
        inv = 1.0 / (total + jnp.concatenate([zero, total3], 1))
        rdot = (rdot + jnp.concatenate([zero, rdot3], 1)) * inv
        wrow[0:1, rows] = rdot
        for u in range(UNITS):
            st[u, 0:1, rows] = part[u] * inv
            st3[u, 0:1, rows3] = part3[u] * inv[:, 128:]

    def grad_scores(u):
        @pl.loop(0, HEADS, unroll=True)
        def _(h):
            at = pl.multiple_of(h * 256, 256)
            rows = pl.ds(at, 256)
            rows3 = pl.ds(pl.multiple_of(h * 128, 128), 128)
            rdot = wrow[0:1, rows]
            pr = prob[u, :, rows] * st[u, 0:1, rows]
            pb[u, :, rows] = pr.astype(BF16)
            dsb[pl.ds(256 * u, 256), rows] = (pr * (gprob[u, :, rows] - rdot)).astype(BF16)
            pr3 = prob3[u, :, rows3] * st3[u, 0:1, rows3]
            p3b[u, :, rows3] = pr3.astype(BF16)
            ds3b[pl.ds(128 * u, 128), rows3] = (
                pr3 * (gprob3[u, :, rows3] - rdot[:, 128:])
            ).astype(BF16)

    def grad_kv(u):
        dv = dot(pb[u], docat[...])
        dv3 = dot(p3b[u], bdo3[...])
        dk = dot(dsb[pl.ds(256 * u, 256), :], qcat[...]) * SCALE
        dk3 = dot(ds3b[pl.ds(128 * u, 128), :], bq3[...]) * SCALE
        for b in range(4):
            for col, big, small in ((0, dk, dk3), (128, dv, dv3)):
                cols = pl.ds(col, 128)
                stage[u, b, 0:64, cols] = big[64 * b : 64 * b + 64].astype(BF16)
                stage[u, b, 64:96, cols] = small[32 * b : 32 * b + 32, :128].astype(BF16)
                stage[u, b, 96:128, cols] = small[32 * b : 32 * b + 32, 128:].astype(BF16)

    back = []

    def part(m):
        return stage.at[m // 4, xor(s, m) % 4]

    def give(m, slot, to):
        cp = remote(part(m), rs.at[slot], rs_send.at[slot], rs_recv.at[slot], seq_dev(to))
        cp.start()
        back.append(cp)

    def landed(slot):
        remote(
            rs.at[slot], rs.at[slot], rs_send.at[slot], rs_recv.at[slot], seq_dev(1)
        ).wait_recv()

    def add(m, *slots):
        total = part(m)[...].astype(F32)
        for slot in slots:
            landed(slot)
            total = total + rs[slot].astype(F32)
        part(m)[...] = total.astype(BF16)

    def grad_queries():
        lane = lax.broadcasted_iota(jnp.int32, (128, 128), 1)
        for h in range(HEADS):
            rows = pl.ds(h * 256, 256)
            rows3 = pl.ds(h * 128, 128)
            dqt = dot(kt[...], dsb[:, rows])
            dqt3 = dot(kt3[...], ds3b[:, rows3])
            right = dqt[:, 128:] + jnp.where(lane < 64, dqt3[:128], dqt3[128:])
            left = dqt[:, :128].T * SCALE
            right = right.T * SCALE
            vec[h] = jnp.sum(left + right, 0, keepdims=True)
            cols = pl.ds(h * DIM, DIM)
            for blk in range(2):
                dqst[blk, 0:64, cols] = left[64 * blk : 64 * blk + 64]
                dqst[blk, 64:96, cols] = right[32 * blk : 32 * blk + 32]
                dqst[blk, 96:128, cols] = right[64 + 32 * blk : 96 + 32 * blk]

    grad_scores(3)
    grad_kv(3)
    give(12, 0, 8)
    give(14, 2, 6)
    give(13, 1, 8)
    give(15, 3, 6)
    for u in (2, 1, 0):
        grad_scores(u)
    grad_queries()
    vec[7] = dot(jnp.ones((8, LANES), BF16), docat[...])[0:1]
    sums = []
    for k in range(8):
        sums.append(
            remote(
                vec.at[xor(s, 2 * k) // 2],
                ar1.at[k, core],
                a_send.at[k],
                a_recv.at[2 * k + core],
                {"seq": xor(s, 2 * k) + 1 - core, "pair": p},
            )
        )
    for k in range(1, 8):
        sums[k].start()

    @pl.when(core == 0)
    def _():
        sums[0].start()

    pair_step = [
        remote(ar2.at[0], ar2.at[n], b_send.at[n], b_recv.at[n], pair_dev(n))
        for n in range(1, pairs)
    ]
    spread = [
        remote(res.at[chip], res.at[chip], c_send.at[m], c_recv.at[m // 2], seq_dev(m))
        for m in range(1, 16)
    ]

    grad_kv(2)
    give(10, 4, 2)
    give(11, 5, 2)

    @pl.when(core == 1)
    def _():
        total = [None, vec[chip]]
        for k in range(8):
            for c in range(2):
                if (k, c) == (0, 1):
                    continue
                remote(
                    ar1.at[k, c], ar1.at[k, c], a_send.at[k], a_recv.at[2 * k + c], seq_dev(1)
                ).wait_recv()
                total[c] = ar1[k, c] if total[c] is None else total[c] + ar1[k, c]
        ar2[0, 0:1] = total[0]
        ar2[0, 1:2] = total[1]
        if pairs > 1:
            pl.semaphore_wait(barrier, pairs - 1)
        for cp in pair_step:
            cp.start()

    grad_kv(1)
    give(6, 6, 6)

    dq_far = remote(
        dqst.at[other], dq_hbm.at[:, own_cols], dq_sem.at[0], dq_sem.at[1], seq_dev(1)
    )
    dq_far.start()
    dq_own = pltpu.make_async_copy(dqst.at[core], dq_hbm.at[:, own_cols], dq_sem.at[2])
    dq_own.start()
    add(4, 0)
    give(4, 7, 6)
    add(5, 1)
    give(5, 8, 2)
    grad_kv(0)
    give(3, 9, 3)
    give(1, 10, 1)

    add(8, 2, 4)
    give(8, 11, 8)
    add(9, 3, 5)
    give(9, 12, 9)
    add(2, 7)
    give(2, 13, 2)
    add(7, 8)
    give(7, 14, 7)

    @pl.when(core == 1)
    def _():
        total = ar2[0]
        for n in range(1, pairs):
            pair_step[n - 1].wait_recv()
            total = total + ar2[n]
        res[chip] = total
        for cp in spread:
            cp.start()

    mine = part(0)[...].astype(F32)
    for slot in (6, 11, 13):
        landed(slot)
        mine = mine + rs[slot].astype(F32)
    theirs = jnp.zeros((128, 256), F32)
    for slot in (10, 9, 12, 14):
        landed(slot)
        theirs = theirs + rs[slot].astype(F32)
    for head, value in ((core, mine), (other, theirs)):
        dkv_ref[:, pl.ds(pl.multiple_of(head * 128, 128), 128)] = value[:, :128]
        dkv_ref[:, pl.ds(pl.multiple_of(256 + head * 128, 128), 128)] = value[:, 128:]

    def rows_from(k):
        at = res.at[xor(s, 2 * k) // 2]
        remote(at, at, c_send.at[k], c_recv.at[k], seq_dev(1)).wait_recv()

    @pl.when(core == 0)
    def _():
        rows_from(0)

    for k in range(1, 8):
        rows_from(k)
    for head in range(2):
        for h in range(HEADS):
            bq_ref[pl.ds((head * HEADS + h) * DIM, DIM)] = res[h, head]
        bv_ref[pl.ds(head * DIM, DIM)] = res[7, head]

    dq_own.wait()
    dq_far.wait_recv()
    dq_far.wait_send()
    qx.wait_send()
    dx.wait_send()
    for cp in list(pushes.values()) + back + sums[1:]:
        cp.wait_send()

    @pl.when(core == 0)
    def _():
        sums[0].wait_send()

    @pl.when(core == 1)
    def _():
        for cp in pair_step + spread:
            cp.wait_send()


def hand_out(*refs):
    ins, outs, sem = refs[:4], refs[4:8], refs[8]
    copies = [pltpu.make_async_copy(a, b, sem.at[i]) for i, (a, b) in enumerate(zip(ins, outs))]
    for cp in copies:
        cp.start()
    for cp in copies:
        cp.wait()


def on_device(pairs, queries, keys_values, cotangent, resp_len, query_bias):
    vm = pltpu.VMEM
    dma = pltpu.SemaphoreType.DMA
    any_spec = pl.BlockSpec(memory_space=pl.ANY)
    hbm_spec = pl.BlockSpec(memory_space=pltpu.HBM)
    vmem_spec = pl.BlockSpec(memory_space=pltpu.VMEM)
    scratch = [
        vm((2, 2, 128, 128), BF16),
        vm((16, 2, 128, 128), BF16),
        vm((2, 128, RLANES), BF16),
        vm((2, 128, RLANES), BF16),
        vm((LANES, 128), BF16),
        vm((LANES, 128), BF16),
        vm((RLANES, 256), BF16),
        vm((RLANES, 256), BF16),
        vm((UNITS, 256, 128), BF16),
        vm((UNITS, 256, 128), BF16),
        vm((UNITS, 128, 256), BF16),
        vm((UNITS, 128, 256), BF16),
        vm((128, UNITS * 256), BF16),
        vm((256, UNITS * 128), BF16),
        vm((256, 128), F32),
        vm((UNITS, 128, 128), F32),
        vm((UNITS, 256, LANES), F32),
        vm((UNITS, 256, LANES), F32),
        vm((UNITS, 128, RLANES), F32),
        vm((UNITS, 128, RLANES), F32),
        vm((UNITS, 8, LANES), F32),
        vm((UNITS, 8, RLANES), F32),
        vm((8, LANES), F32),
        vm((UNITS, 256, LANES), BF16),
        vm((UNITS * 256, LANES), BF16),
        vm((UNITS, 128, RLANES), BF16),
        vm((UNITS * 128, RLANES), BF16),
        vm((UNITS, 4, 128, 256), BF16),
        vm((16, 128, 256), BF16),
        vm((2, 128, RLANES), F32),
        vm((8, 1, 128), F32),
        vm((8, 2, 1, 128), F32),
        vm((pairs, 2, 128), F32),
        vm((8, 2, 128), F32),
        pltpu.SMEM((1, 2), jnp.int32),
        vm((2 * RLANES,), F32),
        dma((8,)),
        dma((16,)),
        dma((16,)),
        dma((2,)),
        dma((2,)),
        dma((16,)),
        dma((16,)),
        dma((3,)),
        dma((8,)),
        dma((16,)),
        dma((pairs,)),
        dma((pairs,)),
        dma((16,)),
        dma((8,)),
        pltpu.SemaphoreType.REGULAR,
    ]
    shapes = (
        jax.ShapeDtypeStruct((128, 2 * RLANES), F32),
        jax.ShapeDtypeStruct((128, 512), F32),
        jax.ShapeDtypeStruct((2 * RLANES,), F32),
        jax.ShapeDtypeStruct((256,), F32),
    )
    made = pl.pallas_call(
        functools.partial(kernel, pairs),
        out_shape=tuple(pltpu.VMEM(a.shape, a.dtype) for a in shapes),
        in_specs=[
            hbm_spec,
            hbm_spec,
            hbm_spec,
            hbm_spec,
            hbm_spec,
        ],
        out_specs=(any_spec, vmem_spec, vmem_spec, vmem_spec),
        scratch_shapes=scratch,
        compiler_params=pltpu.CompilerParams(
            collective_id=0, has_side_effects=True, vmem_limit_bytes=61 * 1024 * 1024
        ),
    )(queries[0], keys_values[0], cotangent[0], resp_len, query_bias)
    dq, dkv, bq, bv = pl.pallas_call(
        hand_out,
        out_shape=shapes,
        in_specs=[any_spec] * 4,
        out_specs=(any_spec,) * 4,
        scratch_shapes=[dma((4,))],
        compiler_params=pltpu.CompilerParams(vmem_limit_bytes=16 * 1024 * 1024),
    )(*made)
    return dq[None], dkv[None], bq, bv


def solution(mesh):
    return jax.shard_map(
        functools.partial(on_device, mesh.shape["pair"]),
        mesh=mesh,
        in_specs=(
            P("pair", "seq", None),
            P("pair", "seq", None),
            P("pair", "seq", None),
            P("pair", None),
            P(),
        ),
        out_specs=(P("pair", "seq", None), P("pair", "seq", None), P(), P()),
        check_vma=False,
    )
```

```python
import functools
import math

import jax
import jax.numpy as jnp
from jax import lax
from jax.experimental import pallas as pl
from jax.experimental.pallas import tpu as pltpu
from jax.sharding import PartitionSpec as P

HEADS = 7
DIM = 128
ROWS = 128
LANES = HEADS * 2 * ROWS
RLANES = HEADS * ROWS
UNITS = 4
SCALE = 1.0 / math.sqrt(DIM)
C2 = SCALE * math.log2(math.e)
NEG = -1e30
MESH = pl.DeviceIdType.MESH
F32, BF16 = jnp.float32, jnp.bfloat16


def xor(value, mask):
    out = value
    bit = 1
    while bit <= mask:
        if mask & bit:
            out = out + bit - 2 * bit * ((value // bit) % 2)
        bit *= 2
    return out


def dot_nt(a, b):
    return lax.dot_general(a, b, (((1,), (1,)), ((), ())), preferred_element_type=F32)


def dot(a, b):
    return jnp.dot(a, b, preferred_element_type=F32)


def kernel(
    pairs,
    q_hbm,
    kv_hbm,
    cot_hbm,
    len_hbm,
    bias_hbm,
    dq_hbm,
    dkv_ref,
    bq_ref,
    bv_ref,
    kvs,
    kvg,
    qin,
    doin,
    qcat,
    docat,
    bq3,
    bdo3,
    kp,
    vp,
    k3,
    v3,
    kt,
    kt3,
    bias12,
    bias3,
    prob,
    gprob,
    prob3,
    gprob3,
    st,
    st3,
    wrow,
    pb,
    dsb,
    p3b,
    ds3b,
    stage,
    rs,
    dqst,
    vec,
    ar1,
    ar2,
    res,
    len_ref,
    bias_ref,
    loc_sem,
    kv_send,
    kv_recv,
    x_send,
    x_recv,
    rs_send,
    rs_recv,
    dq_sem,
    a_send,
    a_recv,
    b_send,
    b_recv,
    c_send,
    c_recv,
    go_sem,
):
    s = lax.axis_index("seq")
    p = lax.axis_index("pair")
    chip = s // 2
    core = s % 2
    other = 1 - core
    duo = s // 4

    def seq_dev(m):
        return {"seq": xor(s, m), "pair": p}

    def pair_dev(n):
        return {"seq": s, "pair": xor(p, n)}

    own_cols = pl.ds(pl.multiple_of(core * RLANES, 128), RLANES)
    other_cols = pl.ds(pl.multiple_of(other * RLANES, 128), RLANES)

    local = []
    for h in range(2):
        for part in range(2):
            local.append(
                pltpu.make_async_copy(
                    kv_hbm.at[:, pl.ds((2 * part + h) * DIM, DIM)],
                    kvs.at[h, part],
                    loc_sem.at[2 * h + part],
                )
            )
    local.append(pltpu.make_async_copy(q_hbm.at[:, own_cols], qin.at[core], loc_sem.at[4]))
    local.append(pltpu.make_async_copy(cot_hbm.at[:, own_cols], doin.at[core], loc_sem.at[5]))
    local.append(pltpu.make_async_copy(bias_hbm, bias_ref, loc_sem.at[6]))
    local.append(pltpu.make_async_copy(len_hbm, len_ref, loc_sem.at[7]))
    for cp in local:
        cp.start()

    barrier = pltpu.get_barrier_semaphore()

    @pl.when(core == 0)
    def _():
        for m in (2, 6, 8):
            pl.semaphore_signal(barrier, inc=1, device_id=seq_dev(m), device_id_type=MESH)

    @pl.when(core == 1)
    def _():
        for m in (3, 7, 9, 1):
            pl.semaphore_signal(barrier, inc=1, device_id=seq_dev(m), device_id_type=MESH)

    for cp in local[:4]:
        cp.wait()

    @pl.when(core == 0)
    def _():
        pl.semaphore_wait(barrier, 7)
        pl.semaphore_signal(go_sem, inc=1, device_id=seq_dev(1), device_id_type=MESH)

    @pl.when(core == 1)
    def _():
        pl.semaphore_wait(go_sem, 1)

    def remote(src, dst, send, recv, dev):
        return pltpu.make_async_remote_copy(
            src_ref=src,
            dst_ref=dst,
            send_sem=send,
            recv_sem=recv,
            device_id=dev,
            device_id_type=MESH,
        )

    pushes = {}

    def push(src, block, mask, to):
        cp = remote(src, kvg.at[block], kv_send.at[mask], kv_recv.at[mask], seq_dev(to))
        cp.start()
        pushes[mask] = cp

    for m in (2, 7, 8, 3, 6, 9, 1):
        push(kvs.at[xor(s, m) % 2], s, m, m)
    qx = remote(q_hbm.at[:, other_cols], qin.at[core], x_send.at[0], x_recv.at[0], seq_dev(1))
    dx = remote(cot_hbm.at[:, other_cols], doin.at[core], x_send.at[1], x_recv.at[1], seq_dev(1))
    qx.start()
    dx.start()

    @pl.when(core == 1)
    def _():
        for n in range(1, pairs):
            pl.semaphore_signal(barrier, inc=1, device_id=pair_dev(n), device_id_type=MESH)

    kvg[s] = kvs[core]

    local[7].wait()
    len0, len1 = len_ref[0, 0], len_ref[0, 1]
    key = lax.broadcasted_iota(jnp.int32, (256, 128), 0)
    lane = lax.broadcasted_iota(jnp.int32, (256, 128), 1)
    bias12[...] = jnp.where(key + 256 * duo <= lane + 128 * chip, 0.0, NEG).astype(F32)
    key = lax.broadcasted_iota(jnp.int32, (128, 128), 0)
    lane = lax.broadcasted_iota(jnp.int32, (128, 128), 1)
    place_q = jnp.where(lane < 64, lane, lane - 64) + 64 * chip
    limit = jnp.where(lane < 64, len0, len1)
    for u in range(UNITS):
        place_k = key + 128 * xor(duo, u)
        seen = (place_k <= place_q) & (place_k < limit)
        bias3[u] = jnp.where(seen, 0.0, NEG).astype(F32)

    bq3[...] = jnp.zeros_like(bq3)
    bdo3[...] = jnp.zeros_like(bdo3)
    row = lax.broadcasted_iota(jnp.int32, (32, 128), 0)

    def prepare(blk):
        base = 32 * (2 * chip + blk)
        for h in range(HEADS):
            cols = pl.ds(h * DIM, DIM)
            bias = bias_ref[pl.ds(pl.multiple_of((core * HEADS + h) * DIM, 128), DIM)][None]
            x = (qin[blk, :, cols].astype(F32) + bias).astype(BF16)
            d = doin[blk, :, cols]
            d1 = jnp.where(row + base < len0, d[64:96].astype(F32), 0.0).astype(BF16)
            d2 = jnp.where(row + base < len1, d[96:128].astype(F32), 0.0).astype(BF16)
            for cat, block, y0, y1, y2 in (
                (qcat, bq3, x[0:64], x[64:96], x[96:128]),
                (docat, bdo3, d[0:64], d1, d2),
            ):
                at = h * 256
                cat[pl.ds(pl.multiple_of(at + 64 * blk, 64), 64), :] = y0
                cat[pl.ds(pl.multiple_of(at + 128 + 32 * blk, 32), 32), :] = y1
                cat[pl.ds(pl.multiple_of(at + 192 + 32 * blk, 32), 32), :] = y2
                block[pl.ds(pl.multiple_of(h * 128 + 32 * blk, 32), 32), pl.ds(0, 128)] = y1
                block[pl.ds(pl.multiple_of(h * 128 + 64 + 32 * blk, 32), 32), pl.ds(128, 128)] = y2

    def relay(held, *ways):
        pushes[held].wait_recv()
        for mask, to in ways:
            push(kvg.at[xor(s, held)], xor(s, held), mask, to)

    relay(2, (4, 6))
    relay(7, (5, 2))
    for k in (4, 5, 6):
        local[k].wait()
    prepare(core)
    relay(8, (10, 2), (14, 6))
    relay(9, (11, 2), (15, 6))
    qx.wait_recv()
    dx.wait_recv()
    prepare(other)
    more = {0: ((3,), (6,), (1,)), 1: ((4, (12, 8)), (5, (13, 8))), 2: ((10,), (11,))}
    more[3] = ((12,), (13,), (14,), (15,))

    def gather_unit(u):
        for way in more[u]:
            relay(*way)
        first = 4 * xor(duo, u)

        def rows(part, start, size):
            return jnp.concatenate(
                [kvg[first + b, part, pl.ds(start, size), :] for b in range(4)], 0
            )

        kp[u] = rows(0, 0, 64)
        vp[u] = rows(1, 0, 64)
        k3[u, :, 0:128] = rows(0, 64, 32)
        k3[u, :, 128:256] = rows(0, 96, 32)
        v3[u, :, 0:128] = rows(1, 64, 32)
        v3[u, :, 128:256] = rows(1, 96, 32)
        kt[:, pl.ds(256 * u, 256)] = kp[u].astype(F32).T.astype(BF16)
        kt3[:, pl.ds(128 * u, 128)] = k3[u].astype(F32).T.astype(BF16)

    def phase_a(u):
        gather_unit(u)
        earlier = xor(duo, u) < duo

        @pl.loop(0, HEADS, unroll=True)
        def _(h):
            at = pl.multiple_of(h * 256, 256)
            at3 = pl.multiple_of(h * 128, 128)
            rows = pl.ds(at, 256)
            rows3 = pl.ds(at3, 128)
            sc = dot_nt(kp[u], qcat[rows, :])
            if u == 0:
                sc = jnp.concatenate([sc[:, :128] + bias12[...], sc[:, 128:]], 1)
            top = jnp.max(sc, 0, keepdims=True)
            pr = jnp.exp2((sc - top) * C2)
            gp = dot_nt(vp[u], docat[rows, :])
            prob[u, :, rows] = pr
            gprob[u, :, rows] = gp
            if u:
                lane1 = lax.broadcasted_iota(jnp.int32, (1, 256), 1)
                top = jnp.where((lane1 >= 128) | earlier, top, NEG)
            st[u, 0:1, rows] = top
            st[u, 1:2, rows] = jnp.sum(pr, 0, keepdims=True)
            st[u, 2:3, rows] = jnp.sum(pr * gp, 0, keepdims=True)

            sc3 = dot_nt(k3[u], bq3[rows3, :]) + bias3[u]
            top3 = jnp.max(sc3, 0, keepdims=True)
            pr3 = jnp.exp2((sc3 - top3) * C2)
            gp3 = dot_nt(v3[u], bdo3[rows3, :])
            prob3[u, :, rows3] = pr3
            gprob3[u, :, rows3] = gp3
            st3[u, 0:1, rows3] = top3
            st3[u, 1:2, rows3] = jnp.sum(pr3, 0, keepdims=True)
            st3[u, 2:3, rows3] = jnp.sum(pr3 * gp3, 0, keepdims=True)

    for u in range(UNITS):
        phase_a(u)

    @pl.loop(0, HEADS)
    def _(h):
        rows = pl.ds(pl.multiple_of(h * 256, 256), 256)
        rows3 = pl.ds(pl.multiple_of(h * 128, 128), 128)
        zero = jnp.zeros((1, 128), F32)
        tops = [st[u, 0:1, rows] for u in range(UNITS)]
        tops3 = [st3[u, 0:1, rows3] for u in range(UNITS)]
        top = functools.reduce(jnp.maximum, tops)
        top_r = functools.reduce(jnp.maximum, tops3, top[:, 128:])
        top = jnp.concatenate([top[:, :128], top_r], 1)
        part = [jnp.exp2((t - top) * C2) for t in tops]
        part3 = [jnp.exp2((t - top_r) * C2) for t in tops3]
        total = sum(st[u, 1:2, rows] * part[u] for u in range(UNITS))
        total3 = sum(st3[u, 1:2, rows3] * part3[u] for u in range(UNITS))
        rdot = sum(st[u, 2:3, rows] * part[u] for u in range(UNITS))
        rdot3 = sum(st3[u, 2:3, rows3] * part3[u] for u in range(UNITS))
        inv = 1.0 / (total + jnp.concatenate([zero, total3], 1))
        rdot = (rdot + jnp.concatenate([zero, rdot3], 1)) * inv
        wrow[0:1, rows] = rdot
        for u in range(UNITS):
            st[u, 0:1, rows] = part[u] * inv
            st3[u, 0:1, rows3] = part3[u] * inv[:, 128:]

    def grad_scores(u):
        @pl.loop(0, HEADS, unroll=True)
        def _(h):
            at = pl.multiple_of(h * 256, 256)
            rows = pl.ds(at, 256)
            rows3 = pl.ds(pl.multiple_of(h * 128, 128), 128)
            rdot = wrow[0:1, rows]
            pr = prob[u, :, rows] * st[u, 0:1, rows]
            pb[u, :, rows] = pr.astype(BF16)
            dsb[pl.ds(256 * u, 256), rows] = (pr * (gprob[u, :, rows] - rdot)).astype(BF16)
            pr3 = prob3[u, :, rows3] * st3[u, 0:1, rows3]
            p3b[u, :, rows3] = pr3.astype(BF16)
            ds3b[pl.ds(128 * u, 128), rows3] = (
                pr3 * (gprob3[u, :, rows3] - rdot[:, 128:])
            ).astype(BF16)

    def grad_kv(u):
        dv = dot(pb[u], docat[...])
        dv3 = dot(p3b[u], bdo3[...])
        dk = dot(dsb[pl.ds(256 * u, 256), :], qcat[...]) * SCALE
        dk3 = dot(ds3b[pl.ds(128 * u, 128), :], bq3[...]) * SCALE
        for b in range(4):
            for col, big, small in ((0, dk, dk3), (128, dv, dv3)):
                cols = pl.ds(col, 128)
                stage[u, b, 0:64, cols] = big[64 * b : 64 * b + 64].astype(BF16)
                stage[u, b, 64:96, cols] = small[32 * b : 32 * b + 32, :128].astype(BF16)
                stage[u, b, 96:128, cols] = small[32 * b : 32 * b + 32, 128:].astype(BF16)

    back = []

    def part(m):
        return stage.at[m // 4, xor(s, m) % 4]

    def give(m, slot, to):
        cp = remote(part(m), rs.at[slot], rs_send.at[slot], rs_recv.at[slot], seq_dev(to))
        cp.start()
        back.append(cp)

    def landed(slot):
        remote(
            rs.at[slot], rs.at[slot], rs_send.at[slot], rs_recv.at[slot], seq_dev(1)
        ).wait_recv()

    def add(m, *slots):
        total = part(m)[...].astype(F32)
        for slot in slots:
            landed(slot)
            total = total + rs[slot].astype(F32)
        part(m)[...] = total.astype(BF16)

    def grad_queries():
        lane = lax.broadcasted_iota(jnp.int32, (128, 128), 1)
        for h in range(HEADS):
            rows = pl.ds(h * 256, 256)
            rows3 = pl.ds(h * 128, 128)
            dqt = dot(kt[...], dsb[:, rows])
            dqt3 = dot(kt3[...], ds3b[:, rows3])
            right = dqt[:, 128:] + jnp.where(lane < 64, dqt3[:128], dqt3[128:])
            left = dqt[:, :128].T * SCALE
            right = right.T * SCALE
            vec[h] = jnp.sum(left + right, 0, keepdims=True)
            cols = pl.ds(h * DIM, DIM)
            for blk in range(2):
                dqst[blk, 0:64, cols] = left[64 * blk : 64 * blk + 64]
                dqst[blk, 64:96, cols] = right[32 * blk : 32 * blk + 32]
                dqst[blk, 96:128, cols] = right[64 + 32 * blk : 96 + 32 * blk]

    for u in reversed(range(UNITS)):
        grad_scores(u)
    grad_queries()
    vec[7] = dot(jnp.ones((8, LANES), BF16), docat[...])[0:1]
    sums = []
    for k in range(8):
        sums.append(
            remote(
                vec.at[xor(s, 2 * k) // 2],
                ar1.at[k, core],
                a_send.at[k],
                a_recv.at[2 * k + core],
                {"seq": xor(s, 2 * k) + 1 - core, "pair": p},
            )
        )
    for k in range(1, 8):
        sums[k].start()

    @pl.when(core == 0)
    def _():
        sums[0].start()

    pair_step = [
        remote(ar2.at[0], ar2.at[n], b_send.at[n], b_recv.at[n], pair_dev(n))
        for n in range(1, pairs)
    ]
    spread = [
        remote(res.at[chip], res.at[chip], c_send.at[m], c_recv.at[m // 2], seq_dev(m))
        for m in range(1, 16)
    ]

    grad_kv(3)
    give(12, 0, 8)
    give(14, 2, 6)
    give(13, 1, 8)
    give(15, 3, 6)

    @pl.when(core == 1)
    def _():
        total = [None, vec[chip]]
        for k in range(8):
            for c in range(2):
                if (k, c) == (0, 1):
                    continue
                remote(
                    ar1.at[k, c], ar1.at[k, c], a_send.at[k], a_recv.at[2 * k + c], seq_dev(1)
                ).wait_recv()
                total[c] = ar1[k, c] if total[c] is None else total[c] + ar1[k, c]
        ar2[0, 0:1] = total[0]
        ar2[0, 1:2] = total[1]
        if pairs > 1:
            pl.semaphore_wait(barrier, pairs - 1)
        for cp in pair_step:
            cp.start()

    grad_kv(2)
    give(10, 4, 2)
    give(11, 5, 2)

    grad_kv(1)
    give(6, 6, 6)

    dq_far = remote(
        dqst.at[other], dq_hbm.at[:, own_cols], dq_sem.at[0], dq_sem.at[1], seq_dev(1)
    )
    dq_far.start()
    dq_own = pltpu.make_async_copy(dqst.at[core], dq_hbm.at[:, own_cols], dq_sem.at[2])
    dq_own.start()
    add(4, 0)
    give(4, 7, 6)
    add(5, 1)
    give(5, 8, 2)
    grad_kv(0)
    give(3, 9, 3)
    give(1, 10, 1)

    add(8, 2, 4)
    give(8, 11, 8)
    add(9, 3, 5)
    give(9, 12, 9)
    add(2, 7)
    give(2, 13, 2)
    add(7, 8)
    give(7, 14, 7)

    @pl.when(core == 1)
    def _():
        total = ar2[0]
        for n in range(1, pairs):
            pair_step[n - 1].wait_recv()
            total = total + ar2[n]
        res[chip] = total
        for cp in spread:
            cp.start()

    mine = part(0)[...].astype(F32)
    for slot in (6, 11, 13):
        landed(slot)
        mine = mine + rs[slot].astype(F32)
    theirs = jnp.zeros((128, 256), F32)
    for slot in (10, 9, 12, 14):
        landed(slot)
        theirs = theirs + rs[slot].astype(F32)
    for head, value in ((core, mine), (other, theirs)):
        dkv_ref[:, pl.ds(pl.multiple_of(head * 128, 128), 128)] = value[:, :128]
        dkv_ref[:, pl.ds(pl.multiple_of(256 + head * 128, 128), 128)] = value[:, 128:]

    def rows_from(k):
        at = res.at[xor(s, 2 * k) // 2]
        remote(at, at, c_send.at[k], c_recv.at[k], seq_dev(1)).wait_recv()

    @pl.when(core == 0)
    def _():
        rows_from(0)

    for k in range(1, 8):
        rows_from(k)
    for head in range(2):
        for h in range(HEADS):
            bq_ref[pl.ds((head * HEADS + h) * DIM, DIM)] = res[h, head]
        bv_ref[pl.ds(head * DIM, DIM)] = res[7, head]

    dq_own.wait()
    dq_far.wait_recv()
    dq_far.wait_send()
    qx.wait_send()
    dx.wait_send()
    for cp in list(pushes.values()) + back + sums[1:]:
        cp.wait_send()

    @pl.when(core == 0)
    def _():
        sums[0].wait_send()

    @pl.when(core == 1)
    def _():
        for cp in pair_step + spread:
            cp.wait_send()


def hand_out(*refs):
    ins, outs, sem = refs[:4], refs[4:8], refs[8]
    copies = [pltpu.make_async_copy(a, b, sem.at[i]) for i, (a, b) in enumerate(zip(ins, outs))]
    for cp in copies:
        cp.start()
    for cp in copies:
        cp.wait()


def on_device(pairs, queries, keys_values, cotangent, resp_len, query_bias):
    vm = pltpu.VMEM
    dma = pltpu.SemaphoreType.DMA
    any_spec = pl.BlockSpec(memory_space=pl.ANY)
    hbm_spec = pl.BlockSpec(memory_space=pltpu.HBM)
    vmem_spec = pl.BlockSpec(memory_space=pltpu.VMEM)
    scratch = [
        vm((2, 2, 128, 128), BF16),
        vm((16, 2, 128, 128), BF16),
        vm((2, 128, RLANES), BF16),
        vm((2, 128, RLANES), BF16),
        vm((LANES, 128), BF16),
        vm((LANES, 128), BF16),
        vm((RLANES, 256), BF16),
        vm((RLANES, 256), BF16),
        vm((UNITS, 256, 128), BF16),
        vm((UNITS, 256, 128), BF16),
        vm((UNITS, 128, 256), BF16),
        vm((UNITS, 128, 256), BF16),
        vm((128, UNITS * 256), BF16),
        vm((256, UNITS * 128), BF16),
        vm((256, 128), F32),
        vm((UNITS, 128, 128), F32),
        vm((UNITS, 256, LANES), F32),
        vm((UNITS, 256, LANES), F32),
        vm((UNITS, 128, RLANES), F32),
        vm((UNITS, 128, RLANES), F32),
        vm((UNITS, 8, LANES), F32),
        vm((UNITS, 8, RLANES), F32),
        vm((8, LANES), F32),
        vm((UNITS, 256, LANES), BF16),
        vm((UNITS * 256, LANES), BF16),
        vm((UNITS, 128, RLANES), BF16),
        vm((UNITS * 128, RLANES), BF16),
        vm((UNITS, 4, 128, 256), BF16),
        vm((16, 128, 256), BF16),
        vm((2, 128, RLANES), F32),
        vm((8, 1, 128), F32),
        vm((8, 2, 1, 128), F32),
        vm((pairs, 2, 128), F32),
        vm((8, 2, 128), F32),
        pltpu.SMEM((1, 2), jnp.int32),
        vm((2 * RLANES,), F32),
        dma((8,)),
        dma((16,)),
        dma((16,)),
        dma((2,)),
        dma((2,)),
        dma((16,)),
        dma((16,)),
        dma((3,)),
        dma((8,)),
        dma((16,)),
        dma((pairs,)),
        dma((pairs,)),
        dma((16,)),
        dma((8,)),
        pltpu.SemaphoreType.REGULAR,
    ]
    shapes = (
        jax.ShapeDtypeStruct((128, 2 * RLANES), F32),
        jax.ShapeDtypeStruct((128, 512), F32),
        jax.ShapeDtypeStruct((2 * RLANES,), F32),
        jax.ShapeDtypeStruct((256,), F32),
    )
    made = pl.pallas_call(
        functools.partial(kernel, pairs),
        out_shape=tuple(pltpu.VMEM(a.shape, a.dtype) for a in shapes),
        in_specs=[
            hbm_spec,
            hbm_spec,
            hbm_spec,
            hbm_spec,
            hbm_spec,
        ],
        out_specs=(any_spec, vmem_spec, vmem_spec, vmem_spec),
        scratch_shapes=scratch,
        compiler_params=pltpu.CompilerParams(
            collective_id=0, has_side_effects=True, vmem_limit_bytes=61 * 1024 * 1024
        ),
    )(queries[0], keys_values[0], cotangent[0], resp_len, query_bias)
    dq, dkv, bq, bv = pl.pallas_call(
        hand_out,
        out_shape=shapes,
        in_specs=[any_spec] * 4,
        out_specs=(any_spec,) * 4,
        scratch_shapes=[dma((4,))],
        compiler_params=pltpu.CompilerParams(vmem_limit_bytes=16 * 1024 * 1024),
    )(*made)
    return dq[None], dkv[None], bq, bv


def solution(mesh):
    return jax.shard_map(
        functools.partial(on_device, mesh.shape["pair"]),
        mesh=mesh,
        in_specs=(
            P("pair", "seq", None),
            P("pair", "seq", None),
            P("pair", "seq", None),
            P("pair", None),
            P(),
        ),
        out_specs=(P("pair", "seq", None), P("pair", "seq", None), P(), P()),
        check_vma=False,
    )
```
